512 devices in a mesh: dp: 8 (over z), expert: 8 (over y_hi, core), etp: 8 (over x, y_lo).
Axes of the slice: x: 4, y: 8 (y_hi: 4, y_lo: 2; y = y_hi * 2 + y_lo), z: 8, core: 2. Of those that a mesh axis runs over, the one named last changes fastest.
Arguments:
- grad_out: bfloat16 [8192, 3072], P(('dp', 'expert'), 'etp'), may hold values from -6 to 6
- routing: int32 [8192, 2], P(('dp', 'expert')), may hold values from 0 to 7, all different within a row; in each aligned block of 128 rows (0 to 127, 128 to 255, ...) at most 48 rows name the same one
- mix_weights: bfloat16 [8192, 2], P(('dp', 'expert')), may hold values from 0.099609375 to 1
- gate_pre: bfloat16 [8, 8, 8, 48, 8192], P('dp', 'expert', None, None, 'etp'), may hold values from -4 to 4
- up_pre: bfloat16 [8, 8, 8, 48, 8192], P('dp', 'expert', None, None, 'etp'), may hold values from -4 to 4
- down_weight: bfloat16 [8, 8192, 3072], P('expert', 'etp', 'dp'), may hold values from -0.0625 to 0.0625
Outputs:
- grad_gate: bfloat16 [8, 8, 8, 48, 8192], P('dp', 'expert', None, None, 'etp')
- grad_up: bfloat16 [8, 8, 8, 48, 8192], P('dp', 'expert', None, None, 'etp')
- grad_mix: float32 [8192, 2], P(('dp', 'expert'))
- grad_down: bfloat16 [8, 8192, 3072], P('expert', 'etp', 'dp')
The draws below stay inside these ranges and needn't reach their ends.
Inputs may be any that keep to these rules, and one draw needn't show every extreme that they name: `routing`: the two experts of a token differ. Within the tokens of one device (aligned blocks of 128 rows) no expert is named more than 48 times, a bound that some block reaches; every expert is named somewhere.
All inputs are finite; a program needn't handle non-finite values.
Results may differ from the reference program's by a relative error of at most 0.0064.
Values may be sent and summed in bfloat16 or wider, within the bound.
A program may use at most 64 MiB of HBM per device.

```python
import math
import jax
import jax.numpy as jnp
import numpy as np
from jax import lax

D = 3072
FF = 8192
TOK_DEV = 128
EXPERTS = 8
GROUPS = 8
CAP = 48
R = 384
TOKENS = 8192


def steps_of(stream_key, dims, split, least, largest):
    factor_of, own = 1.0, jax.random.fold_in(stream_key, 6)
    for dim, blocks in split:
        steps = jnp.exp(jax.random.uniform(jax.random.fold_in(own, dim), (blocks,), jnp.float32, least / len(split), largest / len(split)))
        factor_of = factor_of * jnp.repeat(steps, dims[dim] // blocks).reshape([-1 if axis == dim else 1 for axis in range(len(dims))])
    return factor_of


def shared_out(stream_key, own, number, rows, count, top, most, lean):
    order = jax.random.permutation(stream_key, count)
    crowded, ordinary = portions_of(count, rows * top, most, lean, True), portions_of(count, rows * top, most, lean, False)
    places = jnp.arange(count)

    def named(sizes, turn):
        used = int((sizes > 0).sum())
        fixed = max(1, used // 4)
        passed = fixed + (places - fixed + turn * (used - fixed)) % max(1, count - fixed)
        return jnp.zeros((count,), jnp.int32).at[order[jnp.where(places < fixed, places, passed)]].set(jnp.asarray(sizes, jnp.int32))

    sizes = jnp.where(number % 4 == 0, named(crowded, number // 4), named(ordinary, number - number // 4 - 1))
    mixed = jax.random.permutation(jax.random.fold_in(own, 3), count)
    giver, taker = mixed[0:count // 2 * 2:2], mixed[1:count // 2 * 2:2]
    margin = jnp.minimum(sizes[giver] - 1, most - sizes[taker]) // 2
    margin = jnp.where((giver == order[0]) | (taker == order[0]) | (sizes[taker] == 0), 0, jnp.maximum(margin, 0))
    passed = jax.random.randint(jax.random.fold_in(own, 4), (count // 2,), 0, 1 << 20) % (margin + 1)
    sizes = sizes.at[giver].add(-passed).at[taker].add(passed)
    items = jnp.searchsorted(jnp.cumsum(sizes), jnp.arange(rows * top), side="right").astype(jnp.int32)
    listing = items.reshape(top, rows).T
    listing = listing[jax.random.permutation(jax.random.fold_in(own, 1), rows)]
    turn = jax.random.randint(jax.random.fold_in(own, 2), (rows, 1), 0, top)
    return jnp.take_along_axis(listing, (jnp.arange(top)[None, :] + turn) % top, axis=1)


def portions_of(amount, total, reach, lean, full):
    portions = [(1 << 20) // math.isqrt(rank ** lean) + 1 for rank in range(1, amount + 1)]
    largest = reach if full else min(reach, max(-(-total // amount), total * portions[0] // sum(portions)))
    least = 1 if total - largest >= amount - 1 else 0
    given, rest = [largest] + [least] * (amount - 1), total - largest - least * (amount - 1)
    while rest > 0:
        movable = [i for i in range(1, amount) if given[i] < largest] or [i for i in range(1, amount) if given[i] < reach]
        whole, budget = sum([portions[i] for i in movable]), rest
        for i in movable:
            extra = min(reach - given[i], max(1, budget * portions[i] // whole), rest)
            given[i] = given[i] + extra
            rest = rest - extra
    return np.array(given)


def normal_values(stream_key, extent, width, reach, shards=(), kind=jnp.bfloat16):
    values = jax.random.normal(stream_key, extent, jnp.float32) * width
    if len(shards) > 0:
        values = steps_of(stream_key, extent, shards, -0.22, 0.18) * values
    return jnp.clip(values, min=-reach, max=reach).astype(kind)


def setup_inputs(seed: int = 0) -> dict:
    key_of = jax.random.split(jax.random.key(seed), 7)
    grad_out = normal_values(key_of[0], (TOKENS, D), 1.0, 6.0, ((0, 64), (1, 8)))
    routing_keys = jax.random.split(jax.random.fold_in(key_of[1], 1), TOKENS // TOK_DEV)
    routing_turns = jax.random.permutation(jax.random.fold_in(key_of[1], 3), TOKENS // TOK_DEV)
    routing = jax.vmap(lambda own, number: shared_out(jax.random.fold_in(key_of[1], 2), own, number, TOK_DEV, EXPERTS, 2, CAP, 2))(routing_keys, routing_turns).reshape((TOKENS, 2))
    mix_weights = jnp.clip(0.099609375 + 0.9003906 * jax.random.uniform(key_of[2], (TOKENS, 2), jnp.float32) ** steps_of(key_of[2], (TOKENS, 2), ((0, 64),), -0.2, 0.2), 0.099609375, 1.0).astype(jnp.bfloat16)
    gate_pre = normal_values(key_of[3], (GROUPS, EXPERTS, EXPERTS, CAP, FF), 1.0, 4.0, ((0, 8), (1, 8), (4, 8)))
    up_pre = normal_values(key_of[4], (GROUPS, EXPERTS, EXPERTS, CAP, FF), 1.0, 4.0, ((0, 8), (1, 8), (4, 8)))
    down_weight = normal_values(key_of[5], (EXPERTS, FF, D), FF ** -0.5, 0.0625, ((0, 8), (1, 8), (2, 8)))
    return dict(grad_out=grad_out, routing=routing, mix_weights=mix_weights, gate_pre=gate_pre, up_pre=up_pre, down_weight=down_weight)


def slot_targets(chosen, experts, capacity):
    flattened = chosen.reshape(-1).astype(jnp.int32)
    one_hot = (flattened[:, None] == jnp.arange(experts, dtype=jnp.int32)[None, :]).astype(jnp.int32)
    earlier = jnp.cumsum(one_hot, axis=0) - one_hot
    position = jnp.sum(earlier * one_hot, axis=1)
    return (flattened * capacity + position).astype(jnp.int32)


def swiglu_back(upstream, mix_rows, gate_act, up_act):
    gate_val = gate_act.astype(jnp.float32)
    up_val = up_act.astype(jnp.float32)
    sigmoid_a = jax.nn.sigmoid(gate_val)
    silu_a = gate_val * sigmoid_a
    hidden = silu_a * up_val
    scaled = mix_rows.astype(jnp.float32)[:, None] * upstream
    grad_gate = (scaled * up_val * sigmoid_a * (1.0 + gate_val * (1.0 - sigmoid_a))).astype(jnp.bfloat16)
    grad_up = (scaled * silu_a).astype(jnp.bfloat16)
    row_terms = jnp.sum(upstream * hidden, axis=1)
    return grad_gate, grad_up, row_terms, hidden.astype(jnp.bfloat16)


def weighted_rows(routed, mix_rows):
    return (mix_rows.astype(jnp.float32)[:, None] * routed.astype(jnp.float32)).astype(jnp.bfloat16)


def reference(grad_out, routing, mix_weights, gate_pre, up_pre, down_weight):
    cot_rows = grad_out.reshape(GROUPS, EXPERTS, TOK_DEV, D)
    chosen_all = routing.reshape(GROUPS, EXPERTS, TOK_DEV, 2)
    mix_all = mix_weights.reshape(GROUPS, EXPERTS, TOK_DEV, 2)

    def dispatch(rows_dev, chosen, mixes):
        targets = slot_targets(chosen, EXPERTS, CAP)
        send_rows = jnp.zeros((EXPERTS * CAP, D), jnp.bfloat16).at[targets].set(jnp.repeat(rows_dev, 2, axis=0))
        send_mix = jnp.zeros((EXPERTS * CAP,), jnp.bfloat16).at[targets].set(mixes.reshape(-1))
        return send_rows.reshape(EXPERTS, CAP, D), send_mix.reshape(EXPERTS, CAP)

    sent_rows, sent_mix = jax.vmap(jax.vmap(dispatch))(cot_rows, chosen_all, mix_all)
    received = jnp.swapaxes(sent_rows, 1, 2).reshape(GROUPS, EXPERTS, R, D)
    received_mix = jnp.swapaxes(sent_mix, 1, 2).reshape(GROUPS, EXPERTS, R)
    gate_acts = gate_pre.reshape(GROUPS, EXPERTS, R, FF)
    up_acts = up_pre.reshape(GROUPS, EXPERTS, R, FF)

    def per_expert(index):
        weight = down_weight[index]

        def per_group(accum, group):
            routed = received[group, index]
            mix_rows = received_mix[group, index]
            upstream = lax.dot_general(routed, weight, (((1,), (1,)), ((), ())), preferred_element_type=jnp.float32)
            grad_gate, grad_up, row_terms, hidden_rounded = swiglu_back(upstream, mix_rows, gate_acts[group, index], up_acts[group, index])
            weighted = weighted_rows(routed, mix_rows)
            partial_value = lax.dot_general(hidden_rounded, weighted, (((0,), (0,)), ((), ())), preferred_element_type=jnp.float32).astype(jnp.bfloat16)
            return accum + partial_value.astype(jnp.float32), (grad_gate, grad_up, row_terms)

        accum, outputs = lax.scan(per_group, jnp.zeros((FF, D), jnp.float32), jnp.arange(GROUPS, dtype=jnp.int32))
        return outputs[0], outputs[1], outputs[2], accum.astype(jnp.bfloat16)

    grad_gate, grad_up, row_terms, grad_down = lax.map(per_expert, jnp.arange(EXPERTS, dtype=jnp.int32))
    grad_gate = jnp.swapaxes(grad_gate, 0, 1).reshape(GROUPS, EXPERTS, EXPERTS, CAP, FF)
    grad_up = jnp.swapaxes(grad_up, 0, 1).reshape(GROUPS, EXPERTS, EXPERTS, CAP, FF)
    returned = jnp.swapaxes(row_terms, 0, 1).reshape(GROUPS, EXPERTS, EXPERTS, CAP)
    returned = jnp.swapaxes(returned, 1, 2).reshape(GROUPS, EXPERTS, EXPERTS * CAP)
    targets_all = jax.vmap(jax.vmap(lambda chosen: slot_targets(chosen, EXPERTS, CAP)))(chosen_all)
    grad_mix = jnp.take_along_axis(returned, targets_all, axis=2).reshape(TOKENS, 2)
    return grad_gate, grad_up, grad_mix, grad_down
```

```python
import jax
import jax.numpy as jnp
from jax import lax
from jax.experimental import pallas as pl
from jax.experimental.pallas import tpu as pltpu
from jax.sharding import PartitionSpec as P

N = 8
CAP = 48
R = 384
HID = 1024
C = 384
CH = 256
NCH = 4
TOK = 128
MESH = pl.DeviceIdType.MESH


def copy_to(src, dst, send_sem, recv_sem, axis, index):
    return pltpu.make_async_remote_copy(
        src_ref=src,
        dst_ref=dst,
        send_sem=send_sem,
        recv_sem=recv_sem,
        device_id={axis: index},
        device_id_type=MESH,
    )


def kernel(
    x_ref, rm_ref, gate_hbm, up_hbm, w_hbm,
    gg_hbm, gu_hbm, gm_ref, down_hbm,
    wbuf, abuf, xs, ms, mix, onehot, weighted, a2buf, hbuf, hid, upstream, acc,
    gate, up, gg, gu, down, rts, rtr, gms, gmr,
    io_sem, w_send, w_recv, a1_send, a1_recv, m_send, m_recv, a2_send, a2_recv,
    a3_send, a3_recv, a4_send, a4_recv, h_send, h_recv,
    r1_send, r1_recv, r2_send, r2_recv,
):
    z = lax.axis_index("dp")
    me = lax.axis_index("expert")
    h = lax.axis_index("etp")

    def peer(index, offset):
        return lax.rem(index + offset + N, N)

    barrier = pltpu.get_barrier_semaphore()
    for o in range(1, N):
        for axis, index in (("dp", z), ("expert", me), ("etp", h)):
            pl.semaphore_signal(
                barrier, inc=1, device_id={axis: peer(index, o)}, device_id_type=MESH
            )
    pl.semaphore_wait(barrier, 3 * (N - 1))

    loads = [
        pltpu.make_async_copy(w_hbm, wbuf.at[z], io_sem.at[0]),
        pltpu.make_async_copy(gate_hbm, gate, io_sem.at[1]),
        pltpu.make_async_copy(up_hbm, up, io_sem.at[2]),
    ]
    for load in loads:
        load.start()
    loads[0].wait()

    def ring(buf, send, recv, step, chunk):
        way = 1 if chunk < NCH // 2 else -1
        block = peer(z, -way * step)
        part = buf.at[block, pl.ds(chunk * CH, CH)]
        return copy_to(part, part, send.at[chunk, step], recv.at[chunk, step], "dp", peer(z, way))

    def ring_arrival(buf, send, recv, step, chunk):
        way = 1 if chunk < NCH // 2 else -1
        block = peer(z, -way * (step + 1))
        part = buf.at[block, pl.ds(chunk * CH, CH)]
        return copy_to(part, part, send.at[chunk, step], recv.at[chunk, step], "dp", peer(z, way))

    def forward_w(step):
        for chunk in (0, 2, 1, 3):
            if step > 0:
                ring_arrival(wbuf, w_send, w_recv, step - 1, chunk).wait_recv()
            ring(wbuf, w_send, w_recv, step, chunk).start()

    forward_w(0)

    r0, r1 = rm_ref[0:1, :], rm_ref[1:2, :]
    m0, m1 = rm_ref[2:3, :], rm_ref[3:4, :]
    experts = lax.broadcasted_iota(jnp.int32, (N, TOK), 0).astype(jnp.float32)
    named = jnp.where((r0 == experts) | (r1 == experts), 1.0, 0.0)
    before = jnp.where(
        lax.broadcasted_iota(jnp.int32, (TOK, TOK), 0)
        < lax.broadcasted_iota(jnp.int32, (TOK, TOK), 1),
        1.0,
        0.0,
    ).astype(jnp.bfloat16)
    position = jnp.dot(named.astype(jnp.bfloat16), before, preferred_element_type=jnp.float32)
    place = lax.broadcasted_iota(jnp.int32, (CAP, TOK), 0).astype(jnp.float32)
    for e in range(N):
        chosen = jnp.where(
            (place == position[e : e + 1, :]) & (named[e : e + 1, :] > 0.0), 1.0, 0.0
        )
        onehot[e] = chosen
        weights = jnp.where(r0 == float(e), m0, 0.0) + jnp.where(r1 == float(e), m1, 0.0)
        column = jnp.sum(chosen * weights, axis=1, keepdims=True)
        ms[e] = jnp.broadcast_to(column, (CAP, TOK)).astype(jnp.bfloat16)
        xs[e] = jnp.dot(
            chosen.astype(jnp.bfloat16), x_ref[...], preferred_element_type=jnp.float32
        ).astype(jnp.bfloat16)

    def rows_of(index):
        return pl.ds(pl.multiple_of(index * CAP, CAP), CAP)

    def a1(o, arrival=False):
        dst = peer(me, o)
        where = rows_of(peer(me, -o) if arrival else me)
        return (
            copy_to(xs.at[dst], abuf.at[h, where], a1_send.at[o], a1_recv.at[o], "expert", dst),
            copy_to(ms.at[dst], mix.at[where], m_send.at[o], m_recv.at[o], "expert", dst),
        )

    for o in range(1, N):
        for one in a1(o):
            one.start()
    abuf[h, rows_of(me), :] = xs[me]
    mix[rows_of(me), :] = ms[me]

    forward_w(1)
    for o in range(1, N):
        for one in a1(o, arrival=True):
            one.wait_recv()

    def a2(o, arrival=False):
        slot = peer(h, -o) if arrival else h
        return copy_to(
            abuf.at[slot], abuf.at[slot], a2_send.at[o], a2_recv.at[o], "etp", peer(h, o)
        )

    for o in range(1, N):
        a2(o).start()
    forward_w(2)
    forward_w(3)
    forward_w(4)
    for o in range(1, N):
        a2(o, arrival=True).wait_recv()

    share = mix[rows_of(h), 0:1].astype(jnp.float32)
    for k in range(N):
        weighted[k] = (share * abuf[k, rows_of(h), :].astype(jnp.float32)).astype(jnp.bfloat16)

    def a3(o, arrival=False):
        dst = peer(z, o)
        slot = peer(z, -o) if arrival else z
        return copy_to(
            weighted.at[dst], a2buf.at[slot, rows_of(h)], a3_send.at[o], a3_recv.at[o], "dp", dst
        )

    for o in range(1, N):
        a3(o).start()
    a2buf[z, rows_of(h), :] = weighted[z]
    forward_w(5)
    for o in range(1, N):
        a3(o, arrival=True).wait_recv()

    def a4(o, arrival=False):
        where = rows_of(peer(h, -o) if arrival else h)
        part = a2buf.at[:, where]
        return copy_to(part, part, a4_send.at[o], a4_recv.at[o], "etp", peer(h, o))

    for o in range(1, N):
        a4(o).start()
    forward_w(6)

    def product(block, chunk):
        return lax.dot_general(
            abuf[block],
            wbuf[block, pl.ds(chunk * CH, CH), :],
            (((1,), (1,)), ((), ())),
            preferred_element_type=jnp.float32,
        )

    for chunk in range(NCH):
        way = 1 if chunk < NCH // 2 else -1
        upstream[chunk] = product(z, chunk)

        def add(step, carry, chunk=chunk, way=way):
            upstream[chunk] += product(peer(z, -way * step), chunk)
            return carry

        lax.fori_loop(1, N - 1, add, 0)

    loads[1].wait()
    loads[2].wait()
    RB = 64

    def terms_of(chunk):
        columns = pl.ds(chunk * CH, CH)

        def rows(i, carry):
            where = pl.ds(pl.multiple_of(i * RB, RB), RB)
            a = gate[where, columns].astype(jnp.float32)
            b = up[where, columns].astype(jnp.float32)
            u = upstream[chunk, where, :]
            share = mix[where, 0:1].astype(jnp.float32)
            sig = jax.nn.sigmoid(a)
            silu = a * sig
            hidden = silu * b
            scaled = share * u
            gg[where, columns] = (scaled * b * sig * (1.0 + a * (1.0 - sig))).astype(jnp.bfloat16)
            gu[where, columns] = (scaled * silu).astype(jnp.bfloat16)
            hid[where, :] = hidden.astype(jnp.bfloat16)
            row_sum = jnp.broadcast_to(jnp.sum(u * hidden, axis=1, keepdims=True), (RB, TOK))
            if chunk == 0:
                rts[where, :] = row_sum
            else:
                rts[where, :] += row_sum
            return carry

        lax.fori_loop(0, R // RB, rows, 0)

    for chunk in (0, 2, 1, 3):
        way = 1 if chunk < NCH // 2 else -1
        ring_arrival(wbuf, w_send, w_recv, N - 2, chunk).wait_recv()
        upstream[chunk] += product(peer(z, -way * (N - 1)), chunk)
        terms_of(chunk)
        hbuf[z, pl.ds(chunk * CH, CH), :] = hid[...].T
        ring(hbuf, h_send, h_recv, 0, chunk).start()

    stores = [
        pltpu.make_async_copy(gg, gg_hbm, io_sem.at[3]),
        pltpu.make_async_copy(gu, gu_hbm, io_sem.at[4]),
    ]
    for store in stores:
        store.start()

    def r1_copy(o, arrival=False):
        dst = peer(me, o)
        slot = peer(me, -o) if arrival else me
        return copy_to(
            rts.at[rows_of(dst)], rtr.at[slot], r1_send.at[o], r1_recv.at[o], "expert", dst
        )

    for o in range(1, N):
        r1_copy(o).start()
    rtr[me] = rts[rows_of(me), :]
    for o in range(1, N):
        a4(o, arrival=True).wait_recv()

    def grad(block, chunk):
        return jnp.dot(
            hbuf[block, pl.ds(chunk * CH, CH), :],
            a2buf[block],
            preferred_element_type=jnp.float32,
        )

    for chunk in range(NCH):
        acc[chunk] = grad(z, chunk)
    for o in range(1, N):
        r1_copy(o, arrival=True).wait_recv()
    gm0 = jnp.zeros((1, TOK), jnp.float32)
    gm1 = jnp.zeros((1, TOK), jnp.float32)
    for e in range(N):
        picked = jnp.sum(onehot[e] * rtr[e], axis=0, keepdims=True)
        gm0 += jnp.where(r0 == float(e), picked, 0.0)
        gm1 += jnp.where(r1 == float(e), picked, 0.0)
    row = lax.broadcasted_iota(jnp.int32, (N, TOK), 0)
    gms[...] = jnp.where(row == 0, gm0, jnp.where(row == 1, gm1, 0.0))

    def r2_copy(o, arrival=False):
        slot = peer(h, -o) if arrival else h
        return copy_to(gms, gmr.at[slot], r2_send.at[o], r2_recv.at[o], "etp", peer(h, o))

    for o in range(1, N):
        r2_copy(o).start()
    gmr[h] = gms[...]

    for step in range(1, N):
        for chunk in (0, 2, 1, 3):
            way = 1 if chunk < NCH // 2 else -1
            ring_arrival(hbuf, h_send, h_recv, step - 1, chunk).wait_recv()
            if step < N - 1:
                ring(hbuf, h_send, h_recv, step, chunk).start()
            else:
                down[pl.ds(chunk * CH, CH), :] = (
                    acc[chunk] + grad(peer(z, -way * step), chunk)
                ).astype(jnp.bfloat16)
                pltpu.make_async_copy(
                    down.at[pl.ds(chunk * CH, CH)],
                    down_hbm.at[pl.ds(chunk * CH, CH)],
                    io_sem.at[5 + chunk],
                ).start()
        if step < N - 1:
            for chunk in range(NCH):
                way = 1 if chunk < NCH // 2 else -1
                acc[chunk] += grad(peer(z, -way * step), chunk)
        if step == 1:
            for o in range(1, N):
                r2_copy(o, arrival=True).wait_recv()
            gm_ref[...] = jnp.sum(gmr[...], axis=0)

    for store in stores:
        store.wait()
    for chunk in range(NCH):
        pltpu.make_async_copy(
            down.at[pl.ds(chunk * CH, CH)],
            down_hbm.at[pl.ds(chunk * CH, CH)],
            io_sem.at[5 + chunk],
        ).wait()
    for step in range(N - 1):
        for chunk in range(NCH):
            ring(wbuf, w_send, w_recv, step, chunk).wait_send()
            ring(hbuf, h_send, h_recv, step, chunk).wait_send()
    for o in range(1, N):
        for one in a1(o):
            one.wait_send()
        a2(o).wait_send()
        a3(o).wait_send()
        a4(o).wait_send()
        r1_copy(o).wait_send()
        r2_copy(o).wait_send()


def per_device(grad_out, routing, mix_weights, gate_pre, up_pre, down_weight):
    rm = jnp.concatenate(
        [routing.astype(jnp.float32).T, mix_weights.astype(jnp.float32).T], axis=0
    )
    rm = jnp.pad(rm, ((0, 4), (0, 0)))
    vmem = pl.BlockSpec(memory_space=pltpu.VMEM)
    hbm = pl.BlockSpec(memory_space=pl.ANY)
    bf16, f32 = jnp.bfloat16, jnp.float32
    dma = pltpu.SemaphoreType.DMA
    gg, gu, gm, down = pl.pallas_call(
        kernel,
        out_shape=(
            jax.ShapeDtypeStruct((R, HID), bf16),
            jax.ShapeDtypeStruct((R, HID), bf16),
            jax.ShapeDtypeStruct((N, TOK), f32),
            jax.ShapeDtypeStruct((HID, C), bf16),
        ),
        in_specs=[vmem, vmem, hbm, hbm, hbm],
        out_specs=(hbm, hbm, vmem, hbm),
        scratch_shapes=[
            pltpu.VMEM((N, HID, C), bf16),
            pltpu.VMEM((N, R, C), bf16),
            pltpu.VMEM((N, CAP, C), bf16),
            pltpu.VMEM((N, CAP, TOK), bf16),
            pltpu.VMEM((R, TOK), bf16),
            pltpu.VMEM((N, CAP, TOK), f32),
            pltpu.VMEM((N, CAP, C), bf16),
            pltpu.VMEM((N, R, C), bf16),
            pltpu.VMEM((N, HID, R), bf16),
            pltpu.VMEM((R, CH), bf16),
            pltpu.VMEM((NCH, R, CH), f32),
            pltpu.VMEM((NCH, CH, C), f32),
            pltpu.VMEM((R, HID), bf16),
            pltpu.VMEM((R, HID), bf16),
            pltpu.VMEM((R, HID), bf16),
            pltpu.VMEM((R, HID), bf16),
            pltpu.VMEM((HID, C), bf16),
            pltpu.VMEM((R, TOK), f32),
            pltpu.VMEM((N, CAP, TOK), f32),
            pltpu.VMEM((N, TOK), f32),
            pltpu.VMEM((N, N, TOK), f32),
            dma((9,)),
            dma((NCH, N)), dma((NCH, N)),
            dma((N,)), dma((N,)),
            dma((N,)), dma((N,)),
            dma((N,)), dma((N,)),
            dma((N,)), dma((N,)),
            dma((N,)), dma((N,)),
            dma((NCH, N)), dma((NCH, N)),
            dma((N,)), dma((N,)),
            dma((N,)), dma((N,)),
        ],
        compiler_params=pltpu.CompilerParams(
            collective_id=0, has_side_effects=True, vmem_limit_bytes=56 * 1024 * 1024
        ),
        cost_estimate=pl.CostEstimate(
            flops=4 * R * HID * C * N, bytes_accessed=6 * HID * C * 2, transcendentals=R * HID
        ),
    )(
        grad_out,
        rm,
        gate_pre.reshape(R, HID),
        up_pre.reshape(R, HID),
        down_weight.reshape(HID, C),
    )
    return (
        gg.reshape(gate_pre.shape),
        gu.reshape(gate_pre.shape),
        gm[0:2].T,
        down[None],
    )


def solution(mesh):
    in_specs = (
        P(("dp", "expert"), "etp"),
        P(("dp", "expert"), None),
        P(("dp", "expert"), None),
        P("dp", "expert", None, None, "etp"),
        P("dp", "expert", None, None, "etp"),
        P("expert", "etp", "dp"),
    )
    out_specs = (
        P("dp", "expert", None, None, "etp"),
        P("dp", "expert", None, None, "etp"),
        P(("dp", "expert"), None),
        P("expert", "etp", "dp"),
    )
    return jax.shard_map(
        per_device, mesh=mesh, in_specs=in_specs, out_specs=out_specs, check_vma=False
    )
```

```python
import jax
import jax.numpy as jnp
from jax import lax
from jax.experimental import pallas as pl
from jax.experimental.pallas import tpu as pltpu
from jax.sharding import PartitionSpec as P

N = 8
CAP = 48
R = 384
HID = 1024
C = 384
CH = 256
NCH = 4
SUB = 128
NSUB = 8
SEG = 4
PLANE = (0, 1, 2, 3, 3, 3, 0, 0)
ROLE = (0, 0, 0, 0, 1, 2, 2, 1)
TOK = 128
MESH = pl.DeviceIdType.MESH


def copy_to(src, dst, send_sem, recv_sem, axis, index):
    return pltpu.make_async_remote_copy(
        src_ref=src,
        dst_ref=dst,
        send_sem=send_sem,
        recv_sem=recv_sem,
        device_id={axis: index},
        device_id_type=MESH,
    )


def kernel(
    x_ref, rm_ref, gate_hbm, up_hbm, w_hbm,
    gg_hbm, gu_hbm, gm_ref, down_hbm,
    wbuf, abuf, xs, ms, mix, onehot, weighted, a2buf, hbuf, hid, upstream, acc,
    gate, up, gg, gu, down, psend, precv, rts, rtr, gms, gmr,
    io_sem, w_send, w_recv, a1_send, a1_recv, m_send, m_recv, a2_send, a2_recv,
    a3_send, a3_recv, a4_send, a4_recv, h_send, h_recv,
    p_send, p_recv, r1_send, r1_recv, r2_send, r2_recv,
):
    z = lax.axis_index("dp")
    me = lax.axis_index("expert")
    h = lax.axis_index("etp")

    def peer(index, offset):
        return lax.rem(index + offset + N, N)

    pos = lax.rem(z + 2 * lax.rem(me, 2), SEG)
    start = peer(z, -pos)
    outer = (pos == 0) | (pos == SEG - 1)
    outward = jnp.where(pos == 0, -1, 1)

    barrier = pltpu.get_barrier_semaphore()
    for o in range(1, N):
        for axis, index in (("dp", z), ("expert", me), ("etp", h)):
            pl.semaphore_signal(
                barrier, inc=1, device_id={axis: peer(index, o)}, device_id_type=MESH
            )
    pl.semaphore_wait(barrier, 3 * (N - 1))

    loads = [
        pltpu.make_async_copy(w_hbm, wbuf.at[z], io_sem.at[0]),
        pltpu.make_async_copy(gate_hbm, gate, io_sem.at[1]),
        pltpu.make_async_copy(up_hbm, up, io_sem.at[2]),
    ]
    for load in loads:
        load.start()
    loads[0].wait()

    def ring(buf, send, recv, step, chunk):
        way = 1 if chunk < NCH // 2 else -1
        block = peer(z, -way * step)
        part = buf.at[block, pl.ds(chunk * CH, CH)]
        return copy_to(part, part, send.at[chunk, step], recv.at[chunk, step], "dp", peer(z, way))

    def ring_arrival(buf, send, recv, step, chunk):
        way = 1 if chunk < NCH // 2 else -1
        block = peer(z, -way * (step + 1))
        part = buf.at[block, pl.ds(chunk * CH, CH)]
        return copy_to(part, part, send.at[chunk, step], recv.at[chunk, step], "dp", peer(z, way))

    def forward_w(step):
        for chunk in (0, 2, 1, 3):
            if step > 0:
                ring_arrival(wbuf, w_send, w_recv, step - 1, chunk).wait_recv()
            ring(wbuf, w_send, w_recv, step, chunk).start()

    forward_w(0)

    r0, r1 = rm_ref[0:1, :], rm_ref[1:2, :]
    m0, m1 = rm_ref[2:3, :], rm_ref[3:4, :]
    experts = lax.broadcasted_iota(jnp.int32, (N, TOK), 0).astype(jnp.float32)
    named = jnp.where((r0 == experts) | (r1 == experts), 1.0, 0.0)
    before = jnp.where(
        lax.broadcasted_iota(jnp.int32, (TOK, TOK), 0)
        < lax.broadcasted_iota(jnp.int32, (TOK, TOK), 1),
        1.0,
        0.0,
    ).astype(jnp.bfloat16)
    position = jnp.dot(named.astype(jnp.bfloat16), before, preferred_element_type=jnp.float32)
    place = lax.broadcasted_iota(jnp.int32, (CAP, TOK), 0).astype(jnp.float32)
    for e in range(N):
        chosen = jnp.where(
            (place == position[e : e + 1, :]) & (named[e : e + 1, :] > 0.0), 1.0, 0.0
        )
        onehot[e] = chosen
        weights = jnp.where(r0 == float(e), m0, 0.0) + jnp.where(r1 == float(e), m1, 0.0)
        column = jnp.sum(chosen * weights, axis=1, keepdims=True)
        ms[e] = jnp.broadcast_to(column, (CAP, TOK)).astype(jnp.bfloat16)
        xs[e] = jnp.dot(
            chosen.astype(jnp.bfloat16), x_ref[...], preferred_element_type=jnp.float32
        ).astype(jnp.bfloat16)

    def rows_of(index):
        return pl.ds(pl.multiple_of(index * CAP, CAP), CAP)

    def a1(o, arrival=False):
        dst = peer(me, o)
        where = rows_of(peer(me, -o) if arrival else me)
        return (
            copy_to(xs.at[dst], abuf.at[h, where], a1_send.at[o], a1_recv.at[o], "expert", dst),
            copy_to(ms.at[dst], mix.at[where], m_send.at[o], m_recv.at[o], "expert", dst),
        )

    for o in range(1, N):
        for one in a1(o):
            one.start()
    abuf[h, rows_of(me), :] = xs[me]
    mix[rows_of(me), :] = ms[me]

    forward_w(1)
    for o in range(1, N):
        for one in a1(o, arrival=True):
            one.wait_recv()

    def a2(o, arrival=False):
        slot = peer(h, -o) if arrival else h
        return copy_to(
            abuf.at[slot], abuf.at[slot], a2_send.at[o], a2_recv.at[o], "etp", peer(h, o)
        )

    for o in range(1, N):
        a2(o).start()
    forward_w(2)
    forward_w(3)
    forward_w(4)
    for o in range(1, N):
        a2(o, arrival=True).wait_recv()

    share = mix[rows_of(h), 0:1].astype(jnp.float32)
    for o in range(N):
        weighted[o] = (
            share * abuf[peer(start, o), rows_of(h), :].astype(jnp.float32)
        ).astype(jnp.bfloat16)

    def a3(o):
        return copy_to(
            weighted.at[o],
            a2buf.at[ROLE[o], pos, rows_of(h)],
            a3_send.at[o],
            a3_recv.at[ROLE[o], pos],
            "dp",
            peer(start, PLANE[o]),
        )

    for o in range(N):

        @pl.when(pos != PLANE[o])
        def _(o=o):
            a3(o).start()

        @pl.when(pos == PLANE[o])
        def _(o=o):
            a2buf[ROLE[o], pos, rows_of(h), :] = weighted[o]

    forward_w(5)
    for role in range(3):
        for source in range(SEG):

            @pl.when((pos != source) & ((role == 0) | outer))
            def _(role=role, source=source):
                part = a2buf.at[role, source, rows_of(h)]
                copy_to(
                    part, part, a3_send.at[0], a3_recv.at[role, source], "dp", peer(start, source)
                ).wait_recv()

    def a4(o, role, arrival=False):
        where = rows_of(peer(h, -o) if arrival else h)
        part = a2buf.at[role, :, where]
        return copy_to(
            part, part, a4_send.at[role, o], a4_recv.at[role, o], "etp", peer(h, o)
        )

    def each_a4(act):
        for o in range(1, N):
            act(o, 0)

        @pl.when(outer)
        def _():
            for o in range(1, N):
                act(o, 1)
                act(o, 2)

    each_a4(lambda o, role: a4(o, role).start())
    forward_w(6)

    def product(block, chunk):
        return lax.dot_general(
            abuf[block],
            wbuf[block, pl.ds(chunk * CH, CH), :],
            (((1,), (1,)), ((), ())),
            preferred_element_type=jnp.float32,
        )

    for chunk in range(NCH):
        way = 1 if chunk < NCH // 2 else -1
        upstream[chunk] = product(z, chunk)

        def add(step, carry, chunk=chunk, way=way):
            upstream[chunk] += product(peer(z, -way * step), chunk)
            return carry

        lax.fori_loop(1, N - 1, add, 0)

    loads[1].wait()
    loads[2].wait()
    RB = 64

    def terms_of(chunk):
        columns = pl.ds(chunk * CH, CH)

        def rows(i, carry):
            where = pl.ds(pl.multiple_of(i * RB, RB), RB)
            a = gate[where, columns].astype(jnp.float32)
            b = up[where, columns].astype(jnp.float32)
            u = upstream[chunk, where, :]
            share = mix[where, 0:1].astype(jnp.float32)
            sig = jax.nn.sigmoid(a)
            silu = a * sig
            hidden = silu * b
            scaled = share * u
            gg[where, columns] = (scaled * b * sig * (1.0 + a * (1.0 - sig))).astype(jnp.bfloat16)
            gu[where, columns] = (scaled * silu).astype(jnp.bfloat16)
            hid[where, :] = hidden.astype(jnp.bfloat16)
            row_sum = jnp.broadcast_to(jnp.sum(u * hidden, axis=1, keepdims=True), (RB, TOK))
            if chunk == 0:
                rts[where, :] = row_sum
            else:
                rts[where, :] += row_sum
            return carry

        lax.fori_loop(0, R // RB, rows, 0)

    def h_copy(step, sub, way, arrival=False):
        block = pos - way * (step + 1 if arrival else step)
        part = hbuf.at[block, pl.ds(sub * SUB, SUB)]
        side = 0 if way > 0 else 1
        return copy_to(
            part, part, h_send.at[side, step, sub], h_recv.at[side, step, sub], "dp", peer(z, way)
        )

    def sends(step, way):
        if way > 0:
            return (pos >= step) & (pos < SEG - 1)
        return (pos < SEG - step) & (pos > 0)

    def receives(step, way):
        return (pos > step) if way > 0 else (pos < SEG - 1 - step)

    def h_step(step, sub):
        for way in (1, -1):
            if step > 0:

                @pl.when(receives(step - 1, way))
                def _(way=way):
                    h_copy(step - 1, sub, way, arrival=True).wait_recv()

            if step < SEG - 1:

                @pl.when(sends(step, way))
                def _(way=way):
                    h_copy(step, sub, way).start()

    def grad(role, sub):
        total = None
        for block in range(SEG):
            term = jnp.dot(
                hbuf[block, pl.ds(sub * SUB, SUB), :],
                a2buf[role, block],
                preferred_element_type=jnp.float32,
            )
            total = term if total is None else total + term
        return total

    def partial(role, sub):
        return copy_to(
            psend.at[role - 1, pl.ds(sub * SUB, SUB)],
            precv.at[pl.ds(sub * SUB, SUB)],
            p_send.at[role - 1, sub],
            p_recv.at[sub],
            "dp",
            peer(z, role * outward),
        )

    def finish(sub):
        h_step(SEG - 1, sub)

        @pl.when(outer)
        def _():
            for role in (2, 1):
                psend[role - 1, pl.ds(sub * SUB, SUB), :] = grad(role, sub).astype(jnp.bfloat16)
                partial(role, sub).start()

        acc[sub] = grad(0, sub)

    def store_down(sub):
        where = pl.ds(sub * SUB, SUB)
        return pltpu.make_async_copy(down.at[where], down_hbm.at[where], io_sem.at[5 + sub])

    def conclude(sub):
        partial(1, sub).wait_recv()
        where = pl.ds(sub * SUB, SUB)
        down[where, :] = (acc[sub] + precv[where, :].astype(jnp.float32)).astype(jnp.bfloat16)
        store_down(sub).start()

    order = (0, 2, 1, 3)

    def subs(turn):
        return (2 * order[turn], 2 * order[turn] + 1)

    for turn in range(NCH + SEG):
        if turn < NCH:
            chunk = order[turn]
            way = 1 if chunk < NCH // 2 else -1
            ring_arrival(wbuf, w_send, w_recv, N - 2, chunk).wait_recv()
            upstream[chunk] += product(peer(z, -way * (N - 1)), chunk)
            terms_of(chunk)
            hbuf[pos, pl.ds(chunk * CH, CH), :] = hid[...].T
            for sub in subs(turn):
                h_step(0, sub)
        for step in (1, 2):
            if 0 <= turn - step < NCH:
                for sub in subs(turn - step):
                    h_step(step, sub)
        if turn == SEG - 1:
            stores = [
                pltpu.make_async_copy(gg, gg_hbm, io_sem.at[3]),
                pltpu.make_async_copy(gu, gu_hbm, io_sem.at[4]),
            ]
            for store in stores:
                store.start()

            def r1_copy(o, arrival=False):
                dst = peer(me, o)
                slot = peer(me, -o) if arrival else me
                return copy_to(
                    rts.at[rows_of(dst)], rtr.at[slot], r1_send.at[o], r1_recv.at[o], "expert", dst
                )

            for o in range(1, N):
                r1_copy(o).start()
            rtr[me] = rts[rows_of(me), :]
            each_a4(lambda o, role: a4(o, role, arrival=True).wait_recv())
        if 0 <= turn - 3 < NCH:
            for sub in subs(turn - 3):
                finish(sub)
        if turn == SEG + 1:
            for o in range(1, N):
                r1_copy(o, arrival=True).wait_recv()
            gm0 = jnp.zeros((1, TOK), jnp.float32)
            gm1 = jnp.zeros((1, TOK), jnp.float32)
            for e in range(N):
                picked = jnp.sum(onehot[e] * rtr[e], axis=0, keepdims=True)
                gm0 += jnp.where(r0 == float(e), picked, 0.0)
                gm1 += jnp.where(r1 == float(e), picked, 0.0)
            row = lax.broadcasted_iota(jnp.int32, (N, TOK), 0)
            gms[...] = jnp.where(row == 0, gm0, jnp.where(row == 1, gm1, 0.0))

            def r2_copy(o, arrival=False):
                slot = peer(h, -o) if arrival else h
                return copy_to(gms, gmr.at[slot], r2_send.at[o], r2_recv.at[o], "etp", peer(h, o))

            for o in range(1, N):
                r2_copy(o).start()
            gmr[h] = gms[...]
        if 0 <= turn - 4 < NCH:
            for sub in subs(turn - 4):
                conclude(sub)
    for o in range(1, N):
        r2_copy(o, arrival=True).wait_recv()
    gm_ref[...] = jnp.sum(gmr[...], axis=0)

    for store in stores:
        store.wait()
    for sub in range(NSUB):
        store_down(sub).wait()
        for way in (1, -1):
            for step in range(SEG - 1):

                @pl.when(sends(step, way))
                def _(sub=sub, way=way, step=step):
                    h_copy(step, sub, way).wait_send()

    @pl.when(outer)
    def _():
        for sub in range(NSUB):
            partial(1, sub).wait_send()
            partial(2, sub).wait_send()

    for o in range(N):

        @pl.when(pos != PLANE[o])
        def _(o=o):
            a3(o).wait_send()

    each_a4(lambda o, role: a4(o, role).wait_send())
    for step in range(N - 1):
        for chunk in range(NCH):
            ring(wbuf, w_send, w_recv, step, chunk).wait_send()
    for o in range(1, N):
        for one in a1(o):
            one.wait_send()
        a2(o).wait_send()
        r1_copy(o).wait_send()
        r2_copy(o).wait_send()


def per_device(grad_out, routing, mix_weights, gate_pre, up_pre, down_weight):
    rm = jnp.concatenate(
        [routing.astype(jnp.float32).T, mix_weights.astype(jnp.float32).T], axis=0
    )
    rm = jnp.pad(rm, ((0, 4), (0, 0)))
    vmem = pl.BlockSpec(memory_space=pltpu.VMEM)
    hbm = pl.BlockSpec(memory_space=pl.ANY)
    bf16, f32 = jnp.bfloat16, jnp.float32
    dma = pltpu.SemaphoreType.DMA
    gg, gu, gm, down = pl.pallas_call(
        kernel,
        out_shape=(
            jax.ShapeDtypeStruct((R, HID), bf16),
            jax.ShapeDtypeStruct((R, HID), bf16),
            jax.ShapeDtypeStruct((N, TOK), f32),
            jax.ShapeDtypeStruct((HID, C), bf16),
        ),
        in_specs=[vmem, vmem, hbm, hbm, hbm],
        out_specs=(hbm, hbm, vmem, hbm),
        scratch_shapes=[
            pltpu.VMEM((N, HID, C), bf16),
            pltpu.VMEM((N, R, C), bf16),
            pltpu.VMEM((N, CAP, C), bf16),
            pltpu.VMEM((N, CAP, TOK), bf16),
            pltpu.VMEM((R, TOK), bf16),
            pltpu.VMEM((N, CAP, TOK), f32),
            pltpu.VMEM((N, CAP, C), bf16),
            pltpu.VMEM((3, SEG, R, C), bf16),
            pltpu.VMEM((SEG, HID, R), bf16),
            pltpu.VMEM((R, CH), bf16),
            pltpu.VMEM((NCH, R, CH), f32),
            pltpu.VMEM((NSUB, SUB, C), f32),
            pltpu.VMEM((R, HID), bf16),
            pltpu.VMEM((R, HID), bf16),
            pltpu.VMEM((R, HID), bf16),
            pltpu.VMEM((R, HID), bf16),
            pltpu.VMEM((HID, C), bf16),
            pltpu.VMEM((2, HID, C), bf16),
            pltpu.VMEM((HID, C), bf16),
            pltpu.VMEM((R, TOK), f32),
            pltpu.VMEM((N, CAP, TOK), f32),
            pltpu.VMEM((N, TOK), f32),
            pltpu.VMEM((N, N, TOK), f32),
            dma((5 + NSUB,)),
            dma((NCH, N)), dma((NCH, N)),
            dma((N,)), dma((N,)),
            dma((N,)), dma((N,)),
            dma((N,)), dma((N,)),
            dma((N,)), dma((3, SEG)),
            dma((3, N)), dma((3, N)),
            dma((2, SEG, NSUB)), dma((2, SEG, NSUB)),
            dma((2, NSUB)), dma((NSUB,)),
            dma((N,)), dma((N,)),
            dma((N,)), dma((N,)),
        ],
        compiler_params=pltpu.CompilerParams(
            collective_id=0, has_side_effects=True, vmem_limit_bytes=56 * 1024 * 1024
        ),
        cost_estimate=pl.CostEstimate(
            flops=4 * R * HID * C * N, bytes_accessed=6 * HID * C * 2, transcendentals=R * HID
        ),
    )(
        grad_out,
        rm,
        gate_pre.reshape(R, HID),
        up_pre.reshape(R, HID),
        down_weight.reshape(HID, C),
    )
    return (
        gg.reshape(gate_pre.shape),
        gu.reshape(gate_pre.shape),
        gm[0:2].T,
        down[None],
    )


def solution(mesh):
    in_specs = (
        P(("dp", "expert"), "etp"),
        P(("dp", "expert"), None),
        P(("dp", "expert"), None),
        P("dp", "expert", None, None, "etp"),
        P("dp", "expert", None, None, "etp"),
        P("expert", "etp", "dp"),
    )
    out_specs = (
        P("dp", "expert", None, None, "etp"),
        P("dp", "expert", None, None, "etp"),
        P(("dp", "expert"), None),
        P("expert", "etp", "dp"),
    )
    return jax.shard_map(
        per_device, mesh=mesh, in_specs=in_specs, out_specs=out_specs, check_vma=False
    )
```

```python
import jax
import jax.numpy as jnp
from jax import lax
from jax.experimental import pallas as pl
from jax.experimental.pallas import tpu as pltpu
from jax.sharding import PartitionSpec as P

N = 8
CAP = 48
R = 384
HID = 1024
C = 384
CH = 256
NCH = 4
SUB = 128
NSUB = 8
SEG = 4
PLANE = (0, 1, 2, 3, 3, 3, 0, 0)
ROLE = (0, 0, 0, 0, 1, 2, 2, 1)
TOK = 128
MESH = pl.DeviceIdType.MESH


def copy_to(src, dst, send_sem, recv_sem, axis, index):
    return pltpu.make_async_remote_copy(
        src_ref=src,
        dst_ref=dst,
        send_sem=send_sem,
        recv_sem=recv_sem,
        device_id={axis: index},
        device_id_type=MESH,
    )


def kernel(
    x_ref, chosen_ref, share_ref, gate_hbm, up_hbm, w_hbm,
    gg_hbm, gu_hbm, gm_ref, down_hbm,
    wbuf, arows, abuf, xs, ms, mix, onehot, prow, weighted, a2buf, hbuf, hid, upstream, acc,
    gate, up, gg, gu, down, csend, crecv, psend, precv, rts, rtr, gms, gmr,
    io_sem, w_send, w_recv, a1_send, a1_recv, m_send, m_recv, f_send, f_recv,
    xd_send, xd_recv, xf_send, xf_recv, y_send, y_recv, g_send, g_recv, t_send, t_recv,
    a3_send, a3_recv, b_send, b_recv, a4_send, a4_recv, c_send, c_recv,
    h_send, h_recv, p_send, p_recv, r1_send, r1_recv, r2_send, r2_recv,
):
    z = lax.axis_index("dp")
    me = lax.axis_index("expert")
    h = lax.axis_index("etp")

    def peer(index, offset):
        return lax.rem(index + offset + N, N)

    pos = lax.rem(z + 2 * lax.rem(me, 2), SEG)
    start = peer(z, -pos)
    outer = (pos == 0) | (pos == SEG - 1)
    outward = jnp.where(pos < 2, -1, 1)
    hx = h // 2
    hy = lax.rem(h, 2)
    across = h + 1 - 2 * hy

    def along_x(i):
        return 2 * lax.rem(hx + i, 4) + hy

    barrier = pltpu.get_barrier_semaphore()
    for o in range(1, N):
        for axis, index in (("dp", z), ("expert", me), ("etp", h)):
            pl.semaphore_signal(
                barrier, inc=1, device_id={axis: peer(index, o)}, device_id_type=MESH
            )
    loads = [
        pltpu.make_async_copy(w_hbm, wbuf.at[pos], io_sem.at[0]),
        pltpu.make_async_copy(gate_hbm, gate, io_sem.at[1]),
        pltpu.make_async_copy(up_hbm, up, io_sem.at[2]),
    ]
    for load in loads:
        load.start()

    chosen_experts = chosen_ref[...].astype(jnp.float32)
    shares = share_ref[...].astype(jnp.float32)
    r0, r1 = chosen_experts[0:1, :], chosen_experts[1:2, :]
    m0, m1 = shares[0:1, :], shares[1:2, :]
    experts = lax.broadcasted_iota(jnp.int32, (N, TOK), 0).astype(jnp.float32)
    named = jnp.where((r0 == experts) | (r1 == experts), 1.0, 0.0)
    before = jnp.where(
        lax.broadcasted_iota(jnp.int32, (TOK, TOK), 0)
        < lax.broadcasted_iota(jnp.int32, (TOK, TOK), 1),
        1.0,
        0.0,
    ).astype(jnp.bfloat16)
    position = jnp.dot(named.astype(jnp.bfloat16), before, preferred_element_type=jnp.float32)
    place = lax.broadcasted_iota(jnp.int32, (CAP, TOK), 0).astype(jnp.float32)
    for e in range(N):
        chosen = jnp.where(
            (place == position[e : e + 1, :]) & (named[e : e + 1, :] > 0.0), 1.0, 0.0
        )
        onehot[e] = chosen
        weights = jnp.where(r0 == float(e), m0, 0.0) + jnp.where(r1 == float(e), m1, 0.0)
        column = jnp.sum(chosen * weights, axis=1, keepdims=True)
        ms[e] = jnp.broadcast_to(column, (CAP, TOK)).astype(jnp.bfloat16)
        xs[e] = jnp.dot(
            chosen.astype(jnp.bfloat16), x_ref[...], preferred_element_type=jnp.float32
        ).astype(jnp.bfloat16)

    loads[0].wait()
    pl.semaphore_wait(barrier, 3 * (N - 1))

    def along(bufs, step, part, way, arrival=False):
        buf, send, recv, size = bufs
        block = pos - way * (step + 1 if arrival else step)
        side = 0 if way > 0 else 1
        piece = buf.at[block, pl.ds(part * size, size)]
        return copy_to(
            piece, piece, send.at[side, step, part], recv.at[side, step, part], "dp", peer(z, way)
        )

    def sends(step, way):
        if way > 0:
            return (pos >= step) & (pos < SEG - 1)
        return (pos < SEG - step) & (pos > 0)

    def receives(step, way):
        return (pos > step) if way > 0 else (pos < SEG - 1 - step)

    def along_step(bufs, step, part):
        for way in (1, -1):
            if step > 0:

                @pl.when(receives(step - 1, way))
                def _(way=way):
                    along(bufs, step - 1, part, way, arrival=True).wait_recv()

            if step < SEG - 1:

                @pl.when(sends(step, way))
                def _(way=way):
                    along(bufs, step, part, way).start()

    def along_sent(bufs, parts):
        for way in (1, -1):
            for step in range(SEG - 1):

                @pl.when(sends(step, way))
                def _(way=way, step=step):
                    for part in range(parts):
                        along(bufs, step, part, way).wait_send()

    of_w = (wbuf, w_send, w_recv, CH)
    of_h = (hbuf, h_send, h_recv, SUB)

    along_step(of_w, 0, 0)
    along_step(of_w, 0, 1)

    def rows_of(index):
        return pl.ds(pl.multiple_of(index * CAP, CAP), CAP)

    def a1(o, arrival=False):
        dst = peer(me, o)
        where = rows_of(peer(me, -o) if arrival else me)
        return copy_to(xs.at[dst], arows.at[where], a1_send.at[o], a1_recv.at[o], "expert", dst)

    def m1(o, arrival=False):
        dst = peer(me, o)
        where = rows_of(peer(me, -o) if arrival else me)
        return copy_to(ms.at[dst], mix.at[where], m_send.at[o], m_recv.at[o], "expert", dst)

    for o in range(1, N):
        a1(o).start()
    for o in range(1, N):
        m1(o).start()
    arows[rows_of(me), :] = xs[me]
    mix[rows_of(me), :] = ms[me]

    along_step(of_w, 1, 0)
    for o in range(1, N):
        a1(o, arrival=True).wait_recv()

    def parts(o, arrival=False):
        dst = peer(h, o)
        slot = peer(peer(h, -o) if arrival else h, N - start)
        return copy_to(
            arows.at[rows_of(dst)], prow.at[slot], t_send.at[o], t_recv.at[o], "etp", dst
        )

    for o in range(1, N):
        parts(o).start()
    prow[peer(h, N - start)] = arows[rows_of(h), :]
    along_step(of_w, 0, 2)
    along_step(of_w, 1, 1)
    for o in range(1, N):
        parts(o, arrival=True).wait_recv()

    def abroad():
        role = jnp.where(outer, 1, 2)
        return copy_to(
            prow.at[pl.ds(SEG, SEG)],
            abuf.at[role, :, rows_of(h)],
            f_send.at[0],
            f_recv.at[role],
            "dp",
            peer(z, outward * role),
        )

    def own_x(i, arrival=False):
        where = rows_of(along_x(4 - i) if arrival else h)
        return copy_to(
            prow.at[pl.ds(0, SEG)],
            abuf.at[0, :, where],
            xd_send.at[i],
            xd_recv.at[i],
            "etp",
            along_x(i),
        )

    def own_y(i, arrival=False):
        place = along_x(4 - i)
        piece = abuf.at[0, :, rows_of(place + 1 - 2 * hy if arrival else place)]
        return copy_to(piece, piece, y_send.at[i], y_recv.at[i], "etp", across)

    def pair_y(buf, send, recv, role, arrival=False):
        piece = buf.at[role, :, rows_of(across if arrival else h)]
        return copy_to(piece, piece, send.at[role], recv.at[role], "etp", across)

    def pair_x(buf, send, recv, role, i, arrival=False):
        place = lax.rem(hx + (4 - i if arrival else 0), 4)
        piece = buf.at[role, :, pl.ds(pl.multiple_of(place * 2 * CAP, 2 * CAP), 2 * CAP)]
        return copy_to(
            piece, piece, send.at[role, i], recv.at[role, i], "etp", along_x(i)
        )

    def foreign_y(role, arrival=False):
        return pair_y(abuf, g_send, g_recv, role, arrival)

    def foreign_x(role, side, i, arrival=False):
        place = along_x(4 - i) if arrival else h
        piece = abuf.at[role, :, rows_of(place if side == 0 else place + 1 - 2 * hy)]
        return copy_to(
            piece, piece, xf_send.at[role, side, i], xf_recv.at[role, side, i], "etp", along_x(i)
        )

    abroad().start()
    for i in (2, 1, 3):
        own_x(i).start()
    abuf[0, :, rows_of(h), :] = prow[0:SEG]
    own_y(0).start()
    along_step(of_w, 0, 3)
    along_step(of_w, 1, 2)

    @pl.when(outer)
    def _():
        for role in (2, 1):
            piece = abuf.at[role, :, rows_of(h)]
            copy_to(piece, piece, f_send.at[0], f_recv.at[role], "dp", peer(z, 1)).wait_recv()
            foreign_y(role).start()
            for i in (2, 1, 3):
                foreign_x(role, 0, i).start()

    along_step(of_w, 2, 0)
    for i in (1, 3):
        own_x(i, arrival=True).wait_recv()
        own_y(i).start()

    @pl.when(outer)
    def _():
        for role in (2, 1):
            foreign_y(role, arrival=True).wait_recv()
            for i in (2, 1, 3):
                foreign_x(role, 1, i).start()

    along_step(of_w, 1, 3)
    own_x(2, arrival=True).wait_recv()
    own_y(2).start()
    along_step(of_w, 2, 1)
    for o in range(1, N):
        m1(o, arrival=True).wait_recv()
    share = mix[rows_of(h), 0:1].astype(jnp.float32)
    for o in range(N):
        weighted[o] = (share * prow[o].astype(jnp.float32)).astype(jnp.bfloat16)

    def a3(o):
        return copy_to(
            weighted.at[o],
            a2buf.at[ROLE[o], pos, rows_of(h)],
            a3_send.at[o],
            a3_recv.at[ROLE[o], pos],
            "dp",
            peer(start, PLANE[o]),
        )

    for o in range(N):

        @pl.when(pos != PLANE[o])
        def _(o=o):
            a3(o).start()

        @pl.when(pos == PLANE[o])
        def _(o=o):
            a2buf[ROLE[o], pos, rows_of(h), :] = weighted[o]

    along_step(of_w, 2, 2)
    along_step(of_w, 2, 3)
    for role in range(3):
        for block in range(SEG):

            @pl.when((pos != block) & ((role == 0) | outer))
            def _(role=role, block=block):
                piece = a2buf.at[role, block, rows_of(h)]
                copy_to(
                    piece, piece, a3_send.at[0], a3_recv.at[role, block], "dp", peer(start, block)
                ).wait_recv()

    def a4_y(role, arrival=False):
        return pair_y(a2buf, b_send, b_recv, role, arrival)

    def a4_x(role, i, arrival=False):
        return pair_x(a2buf, a4_send, a4_recv, role, i, arrival)

    def each_role(act):
        act(0)

        @pl.when(outer)
        def _():
            act(1)
            act(2)

    def each_a4_x(act):
        each_role(lambda role: [act(role, i) for i in (1, 2, 3)] and None)

    each_role(lambda role: a4_y(role).start())
    loads[1].wait()
    loads[2].wait()

    def product(role, chunk):
        total = None
        for block in range(SEG):
            term = lax.dot_general(
                abuf[role, block],
                wbuf[block, pl.ds(chunk * CH, CH), :],
                (((1,), (1,)), ((), ())),
                preferred_element_type=jnp.float32,
            )
            total = term if total is None else total + term
        return total

    def c_copy(role, chunk):
        return copy_to(
            csend.at[role - 1, chunk],
            crecv.at[chunk],
            c_send.at[role - 1, chunk],
            c_recv.at[chunk],
            "dp",
            peer(z, role * outward),
        )

    def multiply(role, chunk):
        if role == 0:
            upstream[chunk] = product(0, chunk)
            return

        @pl.when(outer)
        def _():
            csend[role - 1, chunk] = product(role, chunk).astype(jnp.bfloat16)
            c_copy(role, chunk).start()

    def foreign_here(role):
        @pl.when(outer)
        def _():
            for side in (0, 1):
                for i in (1, 2, 3):
                    foreign_x(role, side, i, arrival=True).wait_recv()

    RB = 64

    def terms_of(chunk):
        columns = pl.ds(chunk * CH, CH)

        def rows(i, carry):
            where = pl.ds(pl.multiple_of(i * RB, RB), RB)
            a = gate[where, columns].astype(jnp.float32)
            b = up[where, columns].astype(jnp.float32)
            u = upstream[chunk, where, :] + crecv[chunk, where, :].astype(jnp.float32)
            share = mix[where, 0:1].astype(jnp.float32)
            sig = jax.nn.sigmoid(a)
            silu = a * sig
            hidden = silu * b
            scaled = share * u
            gg[where, columns] = (scaled * b * sig * (1.0 + a * (1.0 - sig))).astype(jnp.bfloat16)
            gu[where, columns] = (scaled * silu).astype(jnp.bfloat16)
            hid[where, :] = hidden.astype(jnp.bfloat16)
            row_sum = jnp.broadcast_to(jnp.sum(u * hidden, axis=1, keepdims=True), (RB, TOK))
            if chunk == 0:
                rts[where, :] = row_sum
            else:
                rts[where, :] += row_sum
            return carry

        lax.fori_loop(0, R // RB, rows, 0)

    def activate(chunk):
        c_copy(1, chunk).wait_recv()
        terms_of(chunk)
        hbuf[pos, pl.ds(chunk * CH, CH), :] = hid[...].T
        for sub in subs(chunk):
            along_step(of_h, 0, sub)

    def grad(role, sub):
        total = None
        for block in range(SEG):
            term = jnp.dot(
                hbuf[block, pl.ds(sub * SUB, SUB), :],
                a2buf[role, block],
                preferred_element_type=jnp.float32,
            )
            total = term if total is None else total + term
        return total

    def partial(role, sub):
        return copy_to(
            psend.at[role - 1, pl.ds(sub * SUB, SUB)],
            precv.at[pl.ds(sub * SUB, SUB)],
            p_send.at[role - 1, sub],
            p_recv.at[sub],
            "dp",
            peer(z, role * outward),
        )

    def finish(sub):
        along_step(of_h, SEG - 1, sub)

        @pl.when(outer)
        def _():
            for role in (2, 1):
                psend[role - 1, pl.ds(sub * SUB, SUB), :] = grad(role, sub).astype(jnp.bfloat16)
                partial(role, sub).start()

        acc[sub] = grad(0, sub)

    def store_down(sub):
        where = pl.ds(sub * SUB, SUB)
        return pltpu.make_async_copy(down.at[where], down_hbm.at[where], io_sem.at[5 + sub])

    def conclude(sub):
        partial(1, sub).wait_recv()
        where = pl.ds(sub * SUB, SUB)
        down[where, :] = (acc[sub] + precv[where, :].astype(jnp.float32)).astype(jnp.bfloat16)
        store_down(sub).start()

    def subs(chunk):
        return (2 * chunk, 2 * chunk + 1)

    def r1_copy(o, arrival=False):
        dst = peer(me, o)
        slot = peer(me, -o) if arrival else me
        return copy_to(
            rts.at[rows_of(dst)], rtr.at[slot], r1_send.at[o], r1_recv.at[o], "expert", dst
        )

    def r2_copy(o, arrival=False):
        slot = peer(h, -o) if arrival else h
        return copy_to(gms, gmr.at[slot], r2_send.at[o], r2_recv.at[o], "etp", peer(h, o))

    stores = [
        pltpu.make_async_copy(gg, gg_hbm, io_sem.at[3]),
        pltpu.make_async_copy(gu, gu_hbm, io_sem.at[4]),
    ]
    for turn in range(NCH + 5):
        if turn == 0:
            along_step(of_w, SEG - 1, 0)
            along_step(of_w, SEG - 1, 1)
            foreign_here(2)
            multiply(2, 0)
            multiply(2, 1)
            for i in range(4):
                own_y(i, arrival=True).wait_recv()
            multiply(0, 0)
            foreign_here(1)
            multiply(1, 0)
            multiply(1, 1)
            multiply(0, 1)
        elif 2 <= turn < NCH:
            along_step(of_w, SEG - 1, turn)
            for role in (2, 1, 0):
                multiply(role, turn)
        if 0 <= turn - 1 < NCH:
            activate(turn - 1)
        for step in (1, 2):
            if 0 <= turn - 1 - step < NCH:
                for sub in subs(turn - 1 - step):
                    along_step(of_h, step, sub)
        if turn == 0:
            each_role(lambda role: a4_y(role, arrival=True).wait_recv())
            each_a4_x(lambda role, i: a4_x(role, i).start())
        if turn == 4:
            each_a4_x(lambda role, i: a4_x(role, i, arrival=True).wait_recv())
            for store in stores:
                store.start()
            for o in range(1, N):
                r1_copy(o).start()
            rtr[me] = rts[rows_of(me), :]
        if 0 <= turn - 4 < NCH:
            for sub in subs(turn - 4):
                finish(sub)
        if turn == 6:
            for o in range(1, N):
                r1_copy(o, arrival=True).wait_recv()
            gm0 = jnp.zeros((1, TOK), jnp.float32)
            gm1 = jnp.zeros((1, TOK), jnp.float32)
            for e in range(N):
                picked = jnp.sum(onehot[e] * rtr[e], axis=0, keepdims=True)
                gm0 += jnp.where(r0 == float(e), picked, 0.0)
                gm1 += jnp.where(r1 == float(e), picked, 0.0)
            row = lax.broadcasted_iota(jnp.int32, (N, TOK), 0)
            gms[...] = jnp.where(row == 0, gm0, jnp.where(row == 1, gm1, 0.0))
            for o in range(1, N):
                r2_copy(o).start()
            gmr[h] = gms[...]
        if 0 <= turn - 5 < NCH:
            for sub in subs(turn - 5):
                conclude(sub)
    for o in range(1, N):
        r2_copy(o, arrival=True).wait_recv()
    gm_ref[...] = jnp.sum(gmr[...], axis=0)[0:2, :]

    for store in stores:
        store.wait()
    for sub in range(NSUB):
        store_down(sub).wait()
    along_sent(of_w, NCH)
    along_sent(of_h, NSUB)

    @pl.when(outer)
    def _():
        for chunk in range(NCH):
            c_copy(1, chunk).wait_send()
            c_copy(2, chunk).wait_send()
        for sub in range(NSUB):
            partial(1, sub).wait_send()
            partial(2, sub).wait_send()

    abroad().wait_send()
    own_y(0).wait_send()
    for i in (1, 2, 3):
        own_x(i).wait_send()
        own_y(i).wait_send()

    @pl.when(outer)
    def _():
        for role in (1, 2):
            foreign_y(role).wait_send()
            for i in (1, 2, 3):
                foreign_x(role, 0, i).wait_send()
                foreign_x(role, 1, i).wait_send()

    for o in range(N):

        @pl.when(pos != PLANE[o])
        def _(o=o):
            a3(o).wait_send()

    each_role(lambda role: a4_y(role).wait_send())
    each_a4_x(lambda role, i: a4_x(role, i).wait_send())
    for o in range(1, N):
        a1(o).wait_send()
        m1(o).wait_send()
        parts(o).wait_send()
        r1_copy(o).wait_send()
        r2_copy(o).wait_send()


def per_device(grad_out, routing, mix_weights, gate_pre, up_pre, down_weight):
    vmem = pl.BlockSpec(memory_space=pltpu.VMEM)
    hbm = pl.BlockSpec(memory_space=pl.ANY)
    bf16, f32 = jnp.bfloat16, jnp.float32
    dma = pltpu.SemaphoreType.DMA
    gg, gu, gm, down = pl.pallas_call(
        kernel,
        out_shape=(
            jax.ShapeDtypeStruct((R, HID), bf16),
            jax.ShapeDtypeStruct((R, HID), bf16),
            jax.ShapeDtypeStruct((2, TOK), f32),
            jax.ShapeDtypeStruct((HID, C), bf16),
        ),
        in_specs=[vmem, vmem, vmem, hbm, hbm, hbm],
        out_specs=(hbm, hbm, vmem, hbm),
        scratch_shapes=[
            pltpu.VMEM((SEG, HID, C), bf16),
            pltpu.VMEM((R, C), bf16),
            pltpu.VMEM((3, SEG, R, C), bf16),
            pltpu.VMEM((N, CAP, C), bf16),
            pltpu.VMEM((N, CAP, TOK), bf16),
            pltpu.VMEM((R, TOK), bf16),
            pltpu.VMEM((N, CAP, TOK), f32),
            pltpu.VMEM((N, CAP, C), bf16),
            pltpu.VMEM((N, CAP, C), bf16),
            pltpu.VMEM((3, SEG, R, C), bf16),
            pltpu.VMEM((SEG, HID, R), bf16),
            pltpu.VMEM((R, CH), bf16),
            pltpu.VMEM((NCH, R, CH), f32),
            pltpu.VMEM((NSUB, SUB, C), f32),
            pltpu.VMEM((R, HID), bf16),
            pltpu.VMEM((R, HID), bf16),
            pltpu.VMEM((R, HID), bf16),
            pltpu.VMEM((R, HID), bf16),
            pltpu.VMEM((HID, C), bf16),
            pltpu.VMEM((2, NCH, R, CH), bf16),
            pltpu.VMEM((NCH, R, CH), bf16),
            pltpu.VMEM((2, HID, C), bf16),
            pltpu.VMEM((HID, C), bf16),
            pltpu.VMEM((R, TOK), f32),
            pltpu.VMEM((N, CAP, TOK), f32),
            pltpu.VMEM((N, TOK), f32),
            pltpu.VMEM((N, N, TOK), f32),
            dma((5 + NSUB,)),
            dma((2, SEG, NCH)), dma((2, SEG, NCH)),
            dma((N,)), dma((N,)),
            dma((N,)), dma((N,)),
            dma((1,)), dma((3,)),
            dma((4,)), dma((4,)),
            dma((3, 2, 4)), dma((3, 2, 4)),
            dma((4,)), dma((4,)),
            dma((3,)), dma((3,)),
            dma((N,)), dma((N,)),
            dma((N,)), dma((3, SEG)),
            dma((3,)), dma((3,)),
            dma((3, 4)), dma((3, 4)),
            dma((2, NCH)), dma((NCH,)),
            dma((2, SEG, NSUB)), dma((2, SEG, NSUB)),
            dma((2, NSUB)), dma((NSUB,)),
            dma((N,)), dma((N,)),
            dma((N,)), dma((N,)),
        ],
        compiler_params=pltpu.CompilerParams(
            collective_id=0, has_side_effects=True, vmem_limit_bytes=56 * 1024 * 1024
        ),
        cost_estimate=pl.CostEstimate(
            flops=4 * R * HID * C * N, bytes_accessed=6 * HID * C * 2, transcendentals=R * HID
        ),
    )(
        grad_out,
        routing.T,
        mix_weights.T,
        gate_pre.reshape(R, HID),
        up_pre.reshape(R, HID),
        down_weight.reshape(HID, C),
    )
    return (
        gg.reshape(gate_pre.shape),
        gu.reshape(gate_pre.shape),
        gm.T,
        down[None],
    )


def solution(mesh):
    in_specs = (
        P(("dp", "expert"), "etp"),
        P(("dp", "expert"), None),
        P(("dp", "expert"), None),
        P("dp", "expert", None, None, "etp"),
        P("dp", "expert", None, None, "etp"),
        P("expert", "etp", "dp"),
    )
    out_specs = (
        P("dp", "expert", None, None, "etp"),
        P("dp", "expert", None, None, "etp"),
        P(("dp", "expert"), None),
        P("expert", "etp", "dp"),
    )
    return jax.shard_map(
        per_device, mesh=mesh, in_specs=in_specs, out_specs=out_specs, check_vma=False
    )
```

```python
import jax
import jax.numpy as jnp
from jax import lax
from jax.experimental import pallas as pl
from jax.experimental.pallas import tpu as pltpu
from jax.sharding import PartitionSpec as P

N = 8
CAP = 48
R = 384
HID = 1024
C = 384
CH = 256
NCH = 4
SEG = 4
TOK = 128
MESH = pl.DeviceIdType.MESH


PLAN = (
    "W0", "W1", "F2", "C20", "C21", "F1", "C10", "C11", "O", "C00",
    "M", "W2", "C22", "C12", "A0", "C01", "W3", "C23", "C13", "A1",
    "C02", "B0", "A2", "C03", "B1", "E0", "A3", "R", "B2", "E1",
    "K0", "B3", "Z", "S", "E2", "K1", "D0", "E3", "K2", "D1",
    "K3", "D2", "D3",
)


def copy_to(src, dst, send_sem, recv_sem, axis, index):
    return pltpu.make_async_remote_copy(
        src_ref=src,
        dst_ref=dst,
        send_sem=send_sem,
        recv_sem=recv_sem,
        device_id={axis: index},
        device_id_type=MESH,
    )


def kernel(
    x_ref, chosen_ref, share_ref, gate_hbm, up_hbm, w_hbm,
    gg_hbm, gu_hbm, gm_ref, down_hbm,
    wbuf, arows, abuf, xs, ms, mix, onehot, prow, hbuf, hid, upstream,
    gate, up, gg, gu, down, csend, crecv, dsend, drecv, rts, rtr, gms, gmr,
    io_sem, w_send, w_recv, a1_send, a1_recv, m_send, m_recv, f_send, f_recv,
    xd_send, xd_recv, xf_send, xf_recv, y_send, y_recv, g_send, g_recv, t_send, t_recv,
    c_send, c_recv, h_send, h_recv, d_send, d_recv, r1_send, r1_recv, r2_send, r2_recv,
):
    z = lax.axis_index("dp")
    me = lax.axis_index("expert")
    h = lax.axis_index("etp")

    def peer(index, offset):
        return lax.rem(index + offset + N, N)

    pos = lax.rem(z + 2 * lax.rem(me, 2), SEG)
    start = peer(z, -pos)
    outer = (pos == 0) | (pos == SEG - 1)
    outward = jnp.where(pos < 2, -1, 1)
    inward = -outward
    hx = h // 2
    hy = lax.rem(h, 2)
    across = h + 1 - 2 * hy

    def along_x(i):
        return 2 * lax.rem(hx + i, 4) + hy

    barrier = pltpu.get_barrier_semaphore()
    for o in range(1, N):
        for axis, index in (("dp", z), ("expert", me), ("etp", h)):
            pl.semaphore_signal(
                barrier, inc=1, device_id={axis: peer(index, o)}, device_id_type=MESH
            )
    loads = [
        pltpu.make_async_copy(w_hbm, wbuf.at[pos], io_sem.at[0]),
        pltpu.make_async_copy(gate_hbm, gate, io_sem.at[1]),
        pltpu.make_async_copy(up_hbm, up, io_sem.at[2]),
    ]
    for load in loads:
        load.start()

    chosen_experts = chosen_ref[...].astype(jnp.float32)
    shares = share_ref[...].astype(jnp.float32)
    r0, r1 = chosen_experts[0:1, :], chosen_experts[1:2, :]
    m0, m1 = shares[0:1, :], shares[1:2, :]
    experts = lax.broadcasted_iota(jnp.int32, (N, TOK), 0).astype(jnp.float32)
    named = jnp.where((r0 == experts) | (r1 == experts), 1.0, 0.0)
    before = jnp.where(
        lax.broadcasted_iota(jnp.int32, (TOK, TOK), 0)
        < lax.broadcasted_iota(jnp.int32, (TOK, TOK), 1),
        1.0,
        0.0,
    ).astype(jnp.bfloat16)
    position = jnp.dot(named.astype(jnp.bfloat16), before, preferred_element_type=jnp.float32)
    place = lax.broadcasted_iota(jnp.int32, (CAP, TOK), 0).astype(jnp.float32)
    for e in range(N):
        chosen = jnp.where(
            (place == position[e : e + 1, :]) & (named[e : e + 1, :] > 0.0), 1.0, 0.0
        )
        onehot[e] = chosen
        weights = jnp.where(r0 == float(e), m0, 0.0) + jnp.where(r1 == float(e), m1, 0.0)
        column = jnp.sum(chosen * weights, axis=1, keepdims=True)
        ms[e] = jnp.broadcast_to(column, (CAP, TOK)).astype(jnp.bfloat16)
        xs[e] = jnp.dot(
            chosen.astype(jnp.bfloat16), x_ref[...], preferred_element_type=jnp.float32
        ).astype(jnp.bfloat16)

    loads[0].wait()
    pl.semaphore_wait(barrier, 3 * (N - 1))

    def along(bufs, step, part, way, arrival=False):
        buf, send, recv, size = bufs
        block = pos - way * (step + 1 if arrival else step)
        side = 0 if way > 0 else 1
        piece = buf.at[block, pl.ds(part * size, size)]
        return copy_to(
            piece, piece, send.at[side, step, part], recv.at[side, step, part], "dp", peer(z, way)
        )

    def sends(step, way):
        if way > 0:
            return (pos >= step) & (pos < SEG - 1)
        return (pos < SEG - step) & (pos > 0)

    def receives(step, way):
        return (pos > step) if way > 0 else (pos < SEG - 1 - step)

    def along_step(bufs, step, part):
        for way in (1, -1):
            if step > 0:

                @pl.when(receives(step - 1, way))
                def _(way=way):
                    along(bufs, step - 1, part, way, arrival=True).wait_recv()

            if step < SEG - 1:

                @pl.when(sends(step, way))
                def _(way=way):
                    along(bufs, step, part, way).start()

    def along_sent(bufs, parts):
        for way in (1, -1):
            for step in range(SEG - 1):

                @pl.when(sends(step, way))
                def _(way=way, step=step):
                    for part in range(parts):
                        along(bufs, step, part, way).wait_send()

    of_w = (wbuf, w_send, w_recv, CH)

    along_step(of_w, 0, 0)
    along_step(of_w, 0, 1)

    def rows_of(index):
        return pl.ds(pl.multiple_of(index * CAP, CAP), CAP)

    def a1(o, arrival=False):
        dst = peer(me, o)
        where = rows_of(peer(me, -o) if arrival else me)
        return copy_to(xs.at[dst], arows.at[where], a1_send.at[o], a1_recv.at[o], "expert", dst)

    def m1(o, arrival=False):
        dst = peer(me, o)
        where = rows_of(peer(me, -o) if arrival else me)
        return copy_to(ms.at[dst], mix.at[where], m_send.at[o], m_recv.at[o], "expert", dst)

    for o in range(1, N):
        a1(o).start()
    for o in range(1, N):
        m1(o).start()
    arows[rows_of(me), :] = xs[me]
    mix[rows_of(me), :] = ms[me]

    along_step(of_w, 1, 0)
    for o in range(1, N):
        a1(o, arrival=True).wait_recv()

    def parts(o, arrival=False):
        dst = peer(h, o)
        slot = peer(peer(h, -o) if arrival else h, N - start)
        return copy_to(
            arows.at[rows_of(dst)], prow.at[slot], t_send.at[o], t_recv.at[o], "etp", dst
        )

    for o in range(1, N):
        parts(o).start()
    prow[peer(h, N - start)] = arows[rows_of(h), :]
    along_step(of_w, 0, 2)
    along_step(of_w, 1, 1)
    for o in range(1, N):
        parts(o, arrival=True).wait_recv()

    def abroad():
        role = jnp.where(outer, 1, 2)
        return copy_to(
            prow.at[pl.ds(SEG, SEG)],
            abuf.at[role, :, rows_of(h)],
            f_send.at[0],
            f_recv.at[role],
            "dp",
            peer(z, outward * role),
        )

    def own_x(i, arrival=False):
        where = rows_of(along_x(4 - i) if arrival else h)
        return copy_to(
            prow.at[pl.ds(0, SEG)],
            abuf.at[0, :, where],
            xd_send.at[i],
            xd_recv.at[i],
            "etp",
            along_x(i),
        )

    def own_y(i, arrival=False):
        place = along_x(4 - i)
        piece = abuf.at[0, :, rows_of(place + 1 - 2 * hy if arrival else place)]
        return copy_to(piece, piece, y_send.at[i], y_recv.at[i], "etp", across)

    def foreign_y(role, arrival=False):
        piece = abuf.at[role, :, rows_of(across if arrival else h)]
        return copy_to(piece, piece, g_send.at[role], g_recv.at[role], "etp", across)

    def foreign_x(role, side, i, arrival=False):
        place = along_x(4 - i) if arrival else h
        piece = abuf.at[role, :, rows_of(place if side == 0 else place + 1 - 2 * hy)]
        return copy_to(
            piece, piece, xf_send.at[role, side, i], xf_recv.at[role, side, i], "etp", along_x(i)
        )

    abroad().start()
    for i in (2, 1, 3):
        own_x(i).start()
    abuf[0, :, rows_of(h), :] = prow[0:SEG]
    own_y(0).start()
    along_step(of_w, 0, 3)
    along_step(of_w, 1, 2)

    @pl.when(outer)
    def _():
        for role in (2, 1):
            piece = abuf.at[role, :, rows_of(h)]
            copy_to(piece, piece, f_send.at[0], f_recv.at[role], "dp", peer(z, 1)).wait_recv()
            foreign_y(role).start()
            for i in (2, 1, 3):
                foreign_x(role, 0, i).start()

    along_step(of_w, 2, 0)
    for i in (1, 3):
        own_x(i, arrival=True).wait_recv()
        own_y(i).start()

    @pl.when(outer)
    def _():
        for role in (2, 1):
            foreign_y(role, arrival=True).wait_recv()
            for i in (2, 1, 3):
                foreign_x(role, 1, i).start()

    along_step(of_w, 1, 3)
    own_x(2, arrival=True).wait_recv()
    own_y(2).start()
    along_step(of_w, 2, 1)
    along_step(of_w, 2, 2)
    along_step(of_w, 2, 3)
    loads[1].wait()
    loads[2].wait()

    def product(role, chunk):
        total = None
        for block in range(SEG):
            term = lax.dot_general(
                abuf[role, block],
                wbuf[block, pl.ds(chunk * CH, CH), :],
                (((1,), (1,)), ((), ())),
                preferred_element_type=jnp.float32,
            )
            total = term if total is None else total + term
        return total

    def c_copy(role, chunk):
        return copy_to(
            csend.at[role - 1, chunk],
            crecv.at[chunk],
            c_send.at[role - 1, chunk],
            c_recv.at[chunk],
            "dp",
            peer(z, role * outward),
        )

    def multiply(role, chunk):
        if role == 0:
            upstream[chunk] = product(0, chunk)
            return

        @pl.when(outer)
        def _():
            csend[role - 1, chunk] = product(role, chunk).astype(jnp.bfloat16)
            c_copy(role, chunk).start()

    def foreign_here(role):
        @pl.when(outer)
        def _():
            for side in (0, 1):
                for i in (1, 2, 3):
                    foreign_x(role, side, i, arrival=True).wait_recv()

    RB = 64

    def terms_of(chunk):
        columns = pl.ds(chunk * CH, CH)

        def rows(i, carry):
            where = pl.ds(pl.multiple_of(i * RB, RB), RB)
            a = gate[where, columns].astype(jnp.float32)
            b = up[where, columns].astype(jnp.float32)
            u = upstream[chunk, where, :] + crecv[chunk, where, :].astype(jnp.float32)
            share = mix[where, 0:1].astype(jnp.float32)
            sig = jax.nn.sigmoid(a)
            silu = a * sig
            hidden = silu * b
            scaled = share * u
            gg[where, columns] = (scaled * b * sig * (1.0 + a * (1.0 - sig))).astype(jnp.bfloat16)
            gu[where, columns] = (scaled * silu).astype(jnp.bfloat16)
            hid[where, :] = (share * hidden).astype(jnp.bfloat16)
            row_sum = jnp.broadcast_to(jnp.sum(u * hidden, axis=1, keepdims=True), (RB, TOK))
            if chunk == 0:
                rts[where, :] = row_sum
            else:
                rts[where, :] += row_sum
            return carry

        lax.fori_loop(0, R // RB, rows, 0)

    def activate(chunk):
        c_copy(1, chunk).wait_recv()
        terms_of(chunk)
        hbuf[0, pl.ds(chunk * CH, CH), :] = hid[...].T
        hidden_abroad(chunk).start()

    def hidden_abroad(chunk):
        role = jnp.where(outer, 1, 2)
        rows = pl.ds(chunk * CH, CH)
        return copy_to(
            hbuf.at[0, rows],
            hbuf.at[role, rows],
            h_send.at[chunk],
            h_recv.at[role, chunk],
            "dp",
            peer(z, outward * role),
        )

    def hidden_here(role, chunk):
        piece = hbuf.at[role, pl.ds(chunk * CH, CH)]
        copy_to(piece, piece, h_send.at[chunk], h_recv.at[role, chunk], "dp", peer(z, 1)).wait_recv()

    def grad(block, chunk, roles):
        total = None
        for role in range(roles):
            term = jnp.dot(
                hbuf[role, pl.ds(chunk * CH, CH), :],
                abuf[role, block],
                preferred_element_type=jnp.float32,
            )
            total = term if total is None else total + term
        return total

    w_in = jnp.where(inward > 0, 0, 1)
    w_out = 1 - w_in

    def sum_on(side, way, block, chunk):
        rows = pl.ds(chunk * CH, CH)
        return copy_to(
            dsend.at[block, rows],
            drecv.at[side, block, rows],
            d_send.at[block, chunk],
            d_recv.at[side, block, chunk],
            "dp",
            peer(z, way),
        )

    def came(side, block, chunk):
        sum_on(side, 1, block, chunk).wait_recv()
        return drecv[side, block, pl.ds(chunk * CH, CH), :].astype(jnp.float32)

    def sums_begin(chunk):
        @pl.when(outer)
        def _():
            hidden_here(1, chunk)
            hidden_here(2, chunk)
            for far in (3, 2, 1):
                block = pos + inward * far
                dsend[block, pl.ds(chunk * CH, CH), :] = grad(block, chunk, 3).astype(jnp.bfloat16)
                sum_on(w_in, inward, block, chunk).start()

    def sums_inward(chunk):
        @pl.when(jnp.logical_not(outer))
        def _():
            for far in (2, 1):
                block = pos + inward * far
                own = grad(block, chunk, 1)
                dsend[block, pl.ds(chunk * CH, CH), :] = (
                    own + came(w_in, block, chunk)
                ).astype(jnp.bfloat16)
                sum_on(w_in, inward, block, chunk).start()

    def sums_outward(chunk):
        @pl.when(jnp.logical_not(outer))
        def _():
            block = pos + outward
            own = grad(block, chunk, 1)
            dsend[block, pl.ds(chunk * CH, CH), :] = (
                own + came(w_out, block, chunk)
            ).astype(jnp.bfloat16)
            sum_on(w_out, outward, block, chunk).start()

    def store_down(chunk):
        rows = pl.ds(chunk * CH, CH)
        return pltpu.make_async_copy(down.at[rows], down_hbm.at[rows], io_sem.at[5 + chunk])

    def conclude(chunk):
        rows = pl.ds(chunk * CH, CH)

        @pl.when(outer)
        def _():
            own = grad(pos, chunk, 3)
            down[rows, :] = (own + came(w_out, pos, chunk)).astype(jnp.bfloat16)

        @pl.when(jnp.logical_not(outer))
        def _():
            own = grad(pos, chunk, 1) + came(w_in, pos, chunk)
            down[rows, :] = (own + came(w_out, pos, chunk)).astype(jnp.bfloat16)

        store_down(chunk).start()

    def r1_copy(o, arrival=False):
        dst = peer(me, o)
        slot = peer(me, -o) if arrival else me
        return copy_to(
            rts.at[rows_of(dst)], rtr.at[slot], r1_send.at[o], r1_recv.at[o], "expert", dst
        )

    def r2_copy(o, arrival=False):
        slot = peer(h, -o) if arrival else h
        return copy_to(gms, gmr.at[slot], r2_send.at[o], r2_recv.at[o], "etp", peer(h, o))

    stores = [
        pltpu.make_async_copy(gg, gg_hbm, io_sem.at[3]),
        pltpu.make_async_copy(gu, gu_hbm, io_sem.at[4]),
    ]
    def row_sums_out():
        for store in stores:
            store.start()
        for o in range(1, N):
            r1_copy(o).start()
        rtr[me] = rts[rows_of(me), :]

    def row_sums_picked():
        for o in range(1, N):
            r1_copy(o, arrival=True).wait_recv()
        gm0 = jnp.zeros((1, TOK), jnp.float32)
        gm1 = jnp.zeros((1, TOK), jnp.float32)
        for e in range(N):
            picked = jnp.sum(onehot[e] * rtr[e], axis=0, keepdims=True)
            gm0 += jnp.where(r0 == float(e), picked, 0.0)
            gm1 += jnp.where(r1 == float(e), picked, 0.0)
        row = lax.broadcasted_iota(jnp.int32, (N, TOK), 0)
        gms[...] = jnp.where(row == 0, gm0, jnp.where(row == 1, gm1, 0.0))
        for o in range(1, N):
            r2_copy(o).start()
        gmr[h] = gms[...]

    def own_here():
        for i in range(4):
            own_y(i, arrival=True).wait_recv()

    def shares_here():
        for o in range(1, N):
            m1(o, arrival=True).wait_recv()

    def early_sent():
        along_sent(of_w, NCH)

        @pl.when(outer)
        def _():
            for chunk in range(NCH):
                c_copy(1, chunk).wait_send()
                c_copy(2, chunk).wait_send()

        abroad().wait_send()
        own_y(0).wait_send()
        for i in (1, 2, 3):
            own_x(i).wait_send()
            own_y(i).wait_send()

        @pl.when(outer)
        def _():
            for role in (1, 2):
                foreign_y(role).wait_send()
                for i in (1, 2, 3):
                    foreign_x(role, 0, i).wait_send()
                    foreign_x(role, 1, i).wait_send()

        for o in range(1, N):
            a1(o).wait_send()
            m1(o).wait_send()
            parts(o).wait_send()

    steps = dict(
        W=lambda chunk: along_step(of_w, SEG - 1, chunk),
        F=foreign_here,
        O=own_here,
        C=multiply,
        A=activate,
        B=sums_begin,
        E=sums_inward,
        K=sums_outward,
        D=conclude,
        M=shares_here,
        R=row_sums_out,
        S=row_sums_picked,
        Z=early_sent,
    )
    for word in PLAN:
        steps[word[0]](*[int(digit) for digit in word[1:]])
    for o in range(1, N):
        r2_copy(o, arrival=True).wait_recv()
    gm_ref[...] = jnp.sum(gmr[...], axis=0)[0:2, :]

    for store in stores:
        store.wait()
    for chunk in range(NCH):
        store_down(chunk).wait()
        hidden_abroad(chunk).wait_send()
        for o in range(1, SEG):
            sum_on(w_in, 1, lax.rem(pos + o, SEG), chunk).wait_send()
    for o in range(1, N):
        r1_copy(o).wait_send()
        r2_copy(o).wait_send()


def hand_out(gg_in, gu_in, down_in, gm_in, gg_out, gu_out, down_out, gm_out, gg, gu, down, sem):
    moves = []
    for array, (src, mid, dst) in enumerate(
        ((gg_in, gg, gg_out), (gu_in, gu, gu_out), (down_in, down, down_out))
    ):
        half = mid.shape[0] // 2
        for part in range(2):
            rows = pl.ds(part * half, half)
            load = pltpu.make_async_copy(src.at[rows], mid.at[rows], sem.at[0, array, part])
            load.start()
            moves.append(
                (load, pltpu.make_async_copy(mid.at[rows], dst.at[rows], sem.at[1, array, part]))
            )
    gm_out[...] = gm_in[...]
    for load, store in moves:
        load.wait()
        store.start()
    for load, store in moves:
        store.wait()


def per_device(grad_out, routing, mix_weights, gate_pre, up_pre, down_weight):
    vmem = pl.BlockSpec(memory_space=pltpu.VMEM)
    hbm = pl.BlockSpec(memory_space=pl.ANY)
    bf16, f32 = jnp.bfloat16, jnp.float32
    dma = pltpu.SemaphoreType.DMA
    gg, gu, gm, down = pl.pallas_call(
        kernel,
        out_shape=(
            jax.ShapeDtypeStruct((R, HID), bf16),
            jax.ShapeDtypeStruct((R, HID), bf16),
            jax.ShapeDtypeStruct((2, TOK), f32),
            jax.ShapeDtypeStruct((HID, C), bf16),
        ),
        in_specs=[vmem, vmem, vmem, hbm, hbm, hbm],
        out_specs=(hbm, hbm, vmem, hbm),
        scratch_shapes=[
            pltpu.VMEM((SEG, HID, C), bf16),
            pltpu.VMEM((R, C), bf16),
            pltpu.VMEM((3, SEG, R, C), bf16),
            pltpu.VMEM((N, CAP, C), bf16),
            pltpu.VMEM((N, CAP, TOK), bf16),
            pltpu.VMEM((R, TOK), bf16),
            pltpu.VMEM((N, CAP, TOK), f32),
            pltpu.VMEM((N, CAP, C), bf16),
            pltpu.VMEM((3, HID, R), bf16),
            pltpu.VMEM((R, CH), bf16),
            pltpu.VMEM((NCH, R, CH), f32),
            pltpu.VMEM((R, HID), bf16),
            pltpu.VMEM((R, HID), bf16),
            pltpu.VMEM((R, HID), bf16),
            pltpu.VMEM((R, HID), bf16),
            pltpu.VMEM((HID, C), bf16),
            pltpu.VMEM((2, NCH, R, CH), bf16),
            pltpu.VMEM((NCH, R, CH), bf16),
            pltpu.VMEM((SEG, HID, C), bf16),
            pltpu.VMEM((2, SEG, HID, C), bf16),
            pltpu.VMEM((R, TOK), f32),
            pltpu.VMEM((N, CAP, TOK), f32),
            pltpu.VMEM((N, TOK), f32),
            pltpu.VMEM((N, N, TOK), f32),
            dma((5 + NCH,)),
            dma((2, SEG, NCH)), dma((2, SEG, NCH)),
            dma((N,)), dma((N,)),
            dma((N,)), dma((N,)),
            dma((1,)), dma((3,)),
            dma((4,)), dma((4,)),
            dma((3, 2, 4)), dma((3, 2, 4)),
            dma((4,)), dma((4,)),
            dma((3,)), dma((3,)),
            dma((N,)), dma((N,)),
            dma((2, NCH)), dma((NCH,)),
            dma((NCH,)), dma((3, NCH)),
            dma((SEG, NCH)), dma((2, SEG, NCH)),
            dma((N,)), dma((N,)),
            dma((N,)), dma((N,)),
        ],
        compiler_params=pltpu.CompilerParams(
            collective_id=0, has_side_effects=True, vmem_limit_bytes=56 * 1024 * 1024
        ),
        cost_estimate=pl.CostEstimate(
            flops=4 * R * HID * C * N, bytes_accessed=6 * HID * C * 2, transcendentals=R * HID
        ),
    )(
        grad_out,
        routing.T,
        mix_weights.T,
        gate_pre.reshape(R, HID),
        up_pre.reshape(R, HID),
        down_weight.reshape(HID, C),
    )
    gg, gu, down, gm = pl.pallas_call(
        hand_out,
        out_shape=(
            jax.ShapeDtypeStruct((R, HID), bf16),
            jax.ShapeDtypeStruct((R, HID), bf16),
            jax.ShapeDtypeStruct((HID, C), bf16),
            jax.ShapeDtypeStruct((2, TOK), f32),
        ),
        in_specs=[hbm, hbm, hbm, vmem],
        out_specs=(hbm, hbm, hbm, vmem),
        scratch_shapes=[
            pltpu.VMEM((R, HID), bf16),
            pltpu.VMEM((R, HID), bf16),
            pltpu.VMEM((HID, C), bf16),
            dma((2, 3, 2)),
        ],
        compiler_params=pltpu.CompilerParams(vmem_limit_bytes=56 * 1024 * 1024),
    )(gg, gu, down, gm)
    return (
        gg.reshape(gate_pre.shape),
        gu.reshape(gate_pre.shape),
        gm.T,
        down[None],
    )


def solution(mesh):
    in_specs = (
        P(("dp", "expert"), "etp"),
        P(("dp", "expert"), None),
        P(("dp", "expert"), None),
        P("dp", "expert", None, None, "etp"),
        P("dp", "expert", None, None, "etp"),
        P("expert", "etp", "dp"),
    )
    out_specs = (
        P("dp", "expert", None, None, "etp"),
        P("dp", "expert", None, None, "etp"),
        P(("dp", "expert"), None),
        P("expert", "etp", "dp"),
    )
    return jax.shard_map(
        per_device, mesh=mesh, in_specs=in_specs, out_specs=out_specs, check_vma=False
    )
```

```python
import jax
import jax.numpy as jnp
from jax import lax
from jax.experimental import pallas as pl
from jax.experimental.pallas import tpu as pltpu
from jax.sharding import PartitionSpec as P

N = 8
CAP = 48
R = 384
HID = 1024
C = 384
CH = 256
NCH = 4
SEG = 4
TOK = 128
MESH = pl.DeviceIdType.MESH


PLAN = (
    "W0", "W1", "F2", "C20", "C21", "F1", "C10", "C11", "O", "C00",
    "M", "W2", "C22", "C12", "A0", "C01", "W3", "C23", "C13", "A1",
    "C02", "B0", "A2", "C03", "B1", "E0", "A3", "R", "B2", "E1",
    "K0", "B3", "Z", "S", "E2", "K1", "D0", "E3", "K2", "D1",
    "K3", "D2", "D3",
)


def copy_to(src, dst, send_sem, recv_sem, axis, index):
    return pltpu.make_async_remote_copy(
        src_ref=src,
        dst_ref=dst,
        send_sem=send_sem,
        recv_sem=recv_sem,
        device_id={axis: index},
        device_id_type=MESH,
    )


def kernel(
    x_ref, chosen_ref, share_ref, gate_hbm, up_hbm, w_hbm,
    gg_hbm, gu_hbm, gm_ref, down_hbm,
    wbuf, arows, abuf, xs, ms, mix, onehot, prow, hbuf, hid, upstream,
    gate, up, gg, gu, down, csend, crecv, dsend, drecv, rts, rtr, gms, gmr,
    io_sem, w_send, w_recv, a1_send, a1_recv, m_send, m_recv, f_send, f_recv,
    xd_send, xd_recv, xf_send, xf_recv, y_send, y_recv, g_send, g_recv, t_send, t_recv,
    c_send, c_recv, h_send, h_recv, d_send, d_recv, r1_send, r1_recv, r2_send, r2_recv,
):
    z = lax.axis_index("dp")
    me = lax.axis_index("expert")
    h = lax.axis_index("etp")

    def peer(index, offset):
        return lax.rem(index + offset + N, N)

    pos = lax.rem(z + 2 * lax.rem(me, 2), SEG)
    start = peer(z, -pos)
    outer = (pos == 0) | (pos == SEG - 1)
    outward = jnp.where(pos < 2, -1, 1)
    inward = -outward
    hx = h // 2
    hy = lax.rem(h, 2)
    across = h + 1 - 2 * hy

    def along_x(i):
        return 2 * lax.rem(hx + i, 4) + hy

    barrier = pltpu.get_barrier_semaphore()
    for o in (1, 2, N - 2, N - 1):
        pl.semaphore_signal(barrier, inc=1, device_id={"dp": peer(z, o)}, device_id_type=MESH)
    for o in range(1, N):
        for axis, index in (("expert", me), ("etp", h)):
            pl.semaphore_signal(
                barrier, inc=1, device_id={axis: peer(index, o)}, device_id_type=MESH
            )
    loads = [
        pltpu.make_async_copy(w_hbm, wbuf.at[pos], io_sem.at[0]),
        pltpu.make_async_copy(gate_hbm, gate, io_sem.at[1]),
        pltpu.make_async_copy(up_hbm, up, io_sem.at[2]),
    ]
    for load in loads:
        load.start()

    chosen_experts = chosen_ref[...].astype(jnp.float32)
    shares = share_ref[...].astype(jnp.float32)
    r0, r1 = chosen_experts[0:1, :], chosen_experts[1:2, :]
    m0, m1 = shares[0:1, :], shares[1:2, :]
    experts = lax.broadcasted_iota(jnp.int32, (N, TOK), 0).astype(jnp.float32)
    named = jnp.where((r0 == experts) | (r1 == experts), 1.0, 0.0)
    before = jnp.where(
        lax.broadcasted_iota(jnp.int32, (TOK, TOK), 0)
        < lax.broadcasted_iota(jnp.int32, (TOK, TOK), 1),
        1.0,
        0.0,
    ).astype(jnp.bfloat16)
    position = jnp.dot(named.astype(jnp.bfloat16), before, preferred_element_type=jnp.float32)
    place = lax.broadcasted_iota(jnp.int32, (CAP, TOK), 0).astype(jnp.float32)
    for e in range(N):
        chosen = jnp.where(
            (place == position[e : e + 1, :]) & (named[e : e + 1, :] > 0.0), 1.0, 0.0
        )
        onehot[e] = chosen
        weights = jnp.where(r0 == float(e), m0, 0.0) + jnp.where(r1 == float(e), m1, 0.0)
        column = jnp.sum(chosen * weights, axis=1, keepdims=True)
        ms[e] = jnp.broadcast_to(column, (CAP, TOK)).astype(jnp.bfloat16)
        xs[e] = jnp.dot(
            chosen.astype(jnp.bfloat16), x_ref[...], preferred_element_type=jnp.float32
        ).astype(jnp.bfloat16)

    loads[0].wait()
    pl.semaphore_wait(barrier, 4 + 2 * (N - 1))

    def along(bufs, step, part, way, arrival=False):
        buf, send, recv, size = bufs
        block = pos - way * (step + 1 if arrival else step)
        side = 0 if way > 0 else 1
        piece = buf.at[block, pl.ds(part * size, size)]
        return copy_to(
            piece, piece, send.at[side, step, part], recv.at[side, step, part], "dp", peer(z, way)
        )

    def sends(step, way):
        if way > 0:
            return (pos >= step) & (pos < SEG - 1)
        return (pos < SEG - step) & (pos > 0)

    def receives(step, way):
        return (pos > step) if way > 0 else (pos < SEG - 1 - step)

    def along_step(bufs, step, part):
        for way in (1, -1):
            if step > 0:

                @pl.when(receives(step - 1, way))
                def _(way=way):
                    along(bufs, step - 1, part, way, arrival=True).wait_recv()

            if step < SEG - 1:

                @pl.when(sends(step, way))
                def _(way=way):
                    along(bufs, step, part, way).start()

    def along_sent(bufs, parts):
        for way in (1, -1):
            for step in range(SEG - 1):

                @pl.when(sends(step, way))
                def _(way=way, step=step):
                    for part in range(parts):
                        along(bufs, step, part, way).wait_send()

    of_w = (wbuf, w_send, w_recv, CH)

    along_step(of_w, 0, 0)
    along_step(of_w, 0, 1)

    def rows_of(index):
        return pl.ds(pl.multiple_of(index * CAP, CAP), CAP)

    def a1(o, arrival=False):
        dst = peer(me, o)
        where = rows_of(peer(me, -o) if arrival else me)
        return copy_to(xs.at[dst], arows.at[where], a1_send.at[o], a1_recv.at[o], "expert", dst)

    def m1(o, arrival=False):
        dst = peer(me, o)
        where = rows_of(peer(me, -o) if arrival else me)
        return copy_to(ms.at[dst], mix.at[where], m_send.at[o], m_recv.at[o], "expert", dst)

    for o in (4, 5, 3, 2, 6, 7, 1):
        a1(o).start()
    for o in range(1, N):
        m1(o).start()
    arows[rows_of(me), :] = xs[me]
    mix[rows_of(me), :] = ms[me]

    along_step(of_w, 1, 0)
    for o in range(1, N):
        a1(o, arrival=True).wait_recv()

    def parts(o, arrival=False):
        dst = peer(h, o)
        slot = peer(peer(h, -o) if arrival else h, N - start)
        return copy_to(
            arows.at[rows_of(dst)], prow.at[slot], t_send.at[o], t_recv.at[o], "etp", dst
        )

    for o in (4, 5, 3, 2, 6, 7, 1):
        parts(o).start()
    prow[peer(h, N - start)] = arows[rows_of(h), :]
    along_step(of_w, 0, 2)
    along_step(of_w, 1, 1)
    for o in range(1, N):
        parts(o, arrival=True).wait_recv()

    def abroad():
        role = jnp.where(outer, 1, 2)
        return copy_to(
            prow.at[pl.ds(SEG, SEG)],
            abuf.at[role, :, rows_of(h)],
            f_send.at[0],
            f_recv.at[role],
            "dp",
            peer(z, outward * role),
        )

    def own_x(i, arrival=False):
        where = rows_of(along_x(4 - i) if arrival else h)
        return copy_to(
            prow.at[pl.ds(0, SEG)],
            abuf.at[0, :, where],
            xd_send.at[i],
            xd_recv.at[i],
            "etp",
            along_x(i),
        )

    def own_y(i, arrival=False):
        place = along_x(4 - i)
        piece = abuf.at[0, :, rows_of(place + 1 - 2 * hy if arrival else place)]
        return copy_to(piece, piece, y_send.at[i], y_recv.at[i], "etp", across)

    def foreign_y(role, arrival=False):
        piece = abuf.at[role, :, rows_of(across if arrival else h)]
        return copy_to(piece, piece, g_send.at[role], g_recv.at[role], "etp", across)

    def foreign_x(role, side, i, arrival=False):
        place = along_x(4 - i) if arrival else h
        piece = abuf.at[role, :, rows_of(place if side == 0 else place + 1 - 2 * hy)]
        return copy_to(
            piece, piece, xf_send.at[role, side, i], xf_recv.at[role, side, i], "etp", along_x(i)
        )

    abroad().start()
    for i in (2, 1, 3):
        own_x(i).start()
    abuf[0, :, rows_of(h), :] = prow[0:SEG]
    own_y(0).start()
    along_step(of_w, 0, 3)
    along_step(of_w, 1, 2)

    @pl.when(outer)
    def _():
        for role in (2, 1):
            piece = abuf.at[role, :, rows_of(h)]
            copy_to(piece, piece, f_send.at[0], f_recv.at[role], "dp", peer(z, 1)).wait_recv()
            foreign_y(role).start()
            for i in (2, 1, 3):
                foreign_x(role, 0, i).start()

    along_step(of_w, 2, 0)
    for i in (1, 3):
        own_x(i, arrival=True).wait_recv()
        own_y(i).start()

    @pl.when(outer)
    def _():
        for role in (2, 1):
            foreign_y(role, arrival=True).wait_recv()
            for i in (2, 1, 3):
                foreign_x(role, 1, i).start()

    along_step(of_w, 1, 3)
    own_x(2, arrival=True).wait_recv()
    own_y(2).start()
    along_step(of_w, 2, 1)
    along_step(of_w, 2, 2)
    along_step(of_w, 2, 3)
    loads[1].wait()
    loads[2].wait()

    def product(role, chunk):
        total = None
        for block in range(SEG):
            term = lax.dot_general(
                abuf[role, block],
                wbuf[block, pl.ds(chunk * CH, CH), :],
                (((1,), (1,)), ((), ())),
                preferred_element_type=jnp.float32,
            )
            total = term if total is None else total + term
        return total

    def c_copy(role, chunk):
        return copy_to(
            csend.at[role - 1, chunk],
            crecv.at[chunk],
            c_send.at[role - 1, chunk],
            c_recv.at[chunk],
            "dp",
            peer(z, role * outward),
        )

    def multiply(role, chunk):
        if role == 0:
            upstream[chunk] = product(0, chunk)
            return

        @pl.when(outer)
        def _():
            csend[role - 1, chunk] = product(role, chunk).astype(jnp.bfloat16)
            c_copy(role, chunk).start()

    def foreign_here(role):
        @pl.when(outer)
        def _():
            for side in (0, 1):
                for i in (1, 2, 3):
                    foreign_x(role, side, i, arrival=True).wait_recv()

    RB = 64

    def terms_of(chunk):
        columns = pl.ds(chunk * CH, CH)

        def rows(i, carry):
            where = pl.ds(pl.multiple_of(i * RB, RB), RB)
            a = gate[where, columns].astype(jnp.float32)
            b = up[where, columns].astype(jnp.float32)
            u = upstream[chunk, where, :] + crecv[chunk, where, :].astype(jnp.float32)
            share = mix[where, 0:1].astype(jnp.float32)
            sig = jax.nn.sigmoid(a)
            silu = a * sig
            hidden = silu * b
            scaled = share * u
            gg[where, columns] = (scaled * b * sig * (1.0 + a * (1.0 - sig))).astype(jnp.bfloat16)
            gu[where, columns] = (scaled * silu).astype(jnp.bfloat16)
            hid[where, :] = (share * hidden).astype(jnp.bfloat16)
            row_sum = jnp.broadcast_to(jnp.sum(u * hidden, axis=1, keepdims=True), (RB, TOK))
            if chunk == 0:
                rts[where, :] = row_sum
            else:
                rts[where, :] += row_sum
            return carry

        lax.fori_loop(0, R // RB, rows, 0)

    def activate(chunk):
        c_copy(1, chunk).wait_recv()
        terms_of(chunk)
        hbuf[0, pl.ds(chunk * CH, CH), :] = hid[...].T
        hidden_abroad(chunk).start()

    def hidden_abroad(chunk):
        role = jnp.where(outer, 1, 2)
        rows = pl.ds(chunk * CH, CH)
        return copy_to(
            hbuf.at[0, rows],
            hbuf.at[role, rows],
            h_send.at[chunk],
            h_recv.at[role, chunk],
            "dp",
            peer(z, outward * role),
        )

    def hidden_here(role, chunk):
        piece = hbuf.at[role, pl.ds(chunk * CH, CH)]
        copy_to(piece, piece, h_send.at[chunk], h_recv.at[role, chunk], "dp", peer(z, 1)).wait_recv()

    def grad(block, chunk, roles):
        total = None
        for role in range(roles):
            term = jnp.dot(
                hbuf[role, pl.ds(chunk * CH, CH), :],
                abuf[role, block],
                preferred_element_type=jnp.float32,
            )
            total = term if total is None else total + term
        return total

    w_in = jnp.where(inward > 0, 0, 1)
    w_out = 1 - w_in

    def sum_on(side, way, block, chunk):
        rows = pl.ds(chunk * CH, CH)
        return copy_to(
            dsend.at[block, rows],
            drecv.at[side, block, rows],
            d_send.at[block, chunk],
            d_recv.at[side, block, chunk],
            "dp",
            peer(z, way),
        )

    def came(side, block, chunk):
        sum_on(side, 1, block, chunk).wait_recv()
        return drecv[side, block, pl.ds(chunk * CH, CH), :].astype(jnp.float32)

    def sums_begin(chunk):
        @pl.when(outer)
        def _():
            hidden_here(1, chunk)
            hidden_here(2, chunk)
            for far in (3, 2, 1):
                block = pos + inward * far
                dsend[block, pl.ds(chunk * CH, CH), :] = grad(block, chunk, 3).astype(jnp.bfloat16)
                sum_on(w_in, inward, block, chunk).start()

    def sums_inward(chunk):
        @pl.when(jnp.logical_not(outer))
        def _():
            for far in (2, 1):
                block = pos + inward * far
                own = grad(block, chunk, 1)
                dsend[block, pl.ds(chunk * CH, CH), :] = (
                    own + came(w_in, block, chunk)
                ).astype(jnp.bfloat16)
                sum_on(w_in, inward, block, chunk).start()

    def sums_outward(chunk):
        @pl.when(jnp.logical_not(outer))
        def _():
            block = pos + outward
            own = grad(block, chunk, 1)
            dsend[block, pl.ds(chunk * CH, CH), :] = (
                own + came(w_out, block, chunk)
            ).astype(jnp.bfloat16)
            sum_on(w_out, outward, block, chunk).start()

    def store_down(chunk):
        rows = pl.ds(chunk * CH, CH)
        return pltpu.make_async_copy(down.at[rows], down_hbm.at[rows], io_sem.at[5 + chunk])

    def conclude(chunk):
        rows = pl.ds(chunk * CH, CH)

        @pl.when(outer)
        def _():
            own = grad(pos, chunk, 3)
            down[rows, :] = (own + came(w_out, pos, chunk)).astype(jnp.bfloat16)

        @pl.when(jnp.logical_not(outer))
        def _():
            own = grad(pos, chunk, 1) + came(w_in, pos, chunk)
            down[rows, :] = (own + came(w_out, pos, chunk)).astype(jnp.bfloat16)

        store_down(chunk).start()

    def r1_copy(o, arrival=False):
        dst = peer(me, o)
        slot = peer(me, -o) if arrival else me
        return copy_to(
            rts.at[rows_of(dst)], rtr.at[slot], r1_send.at[o], r1_recv.at[o], "expert", dst
        )

    def r2_copy(o, arrival=False):
        slot = peer(h, -o) if arrival else h
        return copy_to(gms, gmr.at[slot], r2_send.at[o], r2_recv.at[o], "etp", peer(h, o))

    stores = [
        pltpu.make_async_copy(gg, gg_hbm, io_sem.at[3]),
        pltpu.make_async_copy(gu, gu_hbm, io_sem.at[4]),
    ]
    def row_sums_out():
        for store in stores:
            store.start()
        for o in range(1, N):
            r1_copy(o).start()
        rtr[me] = rts[rows_of(me), :]

    def row_sums_picked():
        for o in range(1, N):
            r1_copy(o, arrival=True).wait_recv()
        gm0 = jnp.zeros((1, TOK), jnp.float32)
        gm1 = jnp.zeros((1, TOK), jnp.float32)
        for e in range(N):
            picked = jnp.sum(onehot[e] * rtr[e], axis=0, keepdims=True)
            gm0 += jnp.where(r0 == float(e), picked, 0.0)
            gm1 += jnp.where(r1 == float(e), picked, 0.0)
        row = lax.broadcasted_iota(jnp.int32, (N, TOK), 0)
        gms[...] = jnp.where(row == 0, gm0, jnp.where(row == 1, gm1, 0.0))
        for o in range(1, N):
            r2_copy(o).start()
        gmr[h] = gms[...]

    def own_here():
        for i in range(4):
            own_y(i, arrival=True).wait_recv()

    def shares_here():
        for o in range(1, N):
            m1(o, arrival=True).wait_recv()

    def early_sent():
        along_sent(of_w, NCH)

        @pl.when(outer)
        def _():
            for chunk in range(NCH):
                c_copy(1, chunk).wait_send()
                c_copy(2, chunk).wait_send()

        abroad().wait_send()
        own_y(0).wait_send()
        for i in (1, 2, 3):
            own_x(i).wait_send()
            own_y(i).wait_send()

        @pl.when(outer)
        def _():
            for role in (1, 2):
                foreign_y(role).wait_send()
                for i in (1, 2, 3):
                    foreign_x(role, 0, i).wait_send()
                    foreign_x(role, 1, i).wait_send()

        for o in range(1, N):
            a1(o).wait_send()
            m1(o).wait_send()
            parts(o).wait_send()

    steps = dict(
        W=lambda chunk: along_step(of_w, SEG - 1, chunk),
        F=foreign_here,
        O=own_here,
        C=multiply,
        A=activate,
        B=sums_begin,
        E=sums_inward,
        K=sums_outward,
        D=conclude,
        M=shares_here,
        R=row_sums_out,
        S=row_sums_picked,
        Z=early_sent,
    )
    for word in PLAN:
        steps[word[0]](*[int(digit) for digit in word[1:]])
    for o in range(1, N):
        r2_copy(o, arrival=True).wait_recv()
    gm_ref[...] = jnp.sum(gmr[...], axis=0)[0:2, :]

    for store in stores:
        store.wait()
    for chunk in range(NCH):
        store_down(chunk).wait()
        hidden_abroad(chunk).wait_send()
        for o in range(1, SEG):
            sum_on(w_in, 1, lax.rem(pos + o, SEG), chunk).wait_send()
    for o in range(1, N):
        r1_copy(o).wait_send()
        r2_copy(o).wait_send()


def hand_out(gg_in, gu_in, down_in, gm_in, gg_out, gu_out, down_out, gm_out, gg, gu, down, sem):
    moves = []
    for array, (src, mid, dst) in enumerate(
        ((gg_in, gg, gg_out), (gu_in, gu, gu_out), (down_in, down, down_out))
    ):
        half = mid.shape[0] // 2
        for part in range(2):
            rows = pl.ds(part * half, half)
            load = pltpu.make_async_copy(src.at[rows], mid.at[rows], sem.at[0, array, part])
            load.start()
            moves.append(
                (load, pltpu.make_async_copy(mid.at[rows], dst.at[rows], sem.at[1, array, part]))
            )
    gm_out[...] = gm_in[...]
    for load, store in moves:
        load.wait()
        store.start()
    for load, store in moves:
        store.wait()


def per_device(grad_out, routing, mix_weights, gate_pre, up_pre, down_weight):
    vmem = pl.BlockSpec(memory_space=pltpu.VMEM)
    hbm = pl.BlockSpec(memory_space=pl.ANY)
    bf16, f32 = jnp.bfloat16, jnp.float32
    dma = pltpu.SemaphoreType.DMA
    gg, gu, gm, down = pl.pallas_call(
        kernel,
        out_shape=(
            jax.ShapeDtypeStruct((R, HID), bf16),
            jax.ShapeDtypeStruct((R, HID), bf16),
            jax.ShapeDtypeStruct((2, TOK), f32),
            jax.ShapeDtypeStruct((HID, C), bf16),
        ),
        in_specs=[vmem, vmem, vmem, hbm, hbm, hbm],
        out_specs=(hbm, hbm, vmem, hbm),
        scratch_shapes=[
            pltpu.VMEM((SEG, HID, C), bf16),
            pltpu.VMEM((R, C), bf16),
            pltpu.VMEM((3, SEG, R, C), bf16),
            pltpu.VMEM((N, CAP, C), bf16),
            pltpu.VMEM((N, CAP, TOK), bf16),
            pltpu.VMEM((R, TOK), bf16),
            pltpu.VMEM((N, CAP, TOK), f32),
            pltpu.VMEM((N, CAP, C), bf16),
            pltpu.VMEM((3, HID, R), bf16),
            pltpu.VMEM((R, CH), bf16),
            pltpu.VMEM((NCH, R, CH), f32),
            pltpu.VMEM((R, HID), bf16),
            pltpu.VMEM((R, HID), bf16),
            pltpu.VMEM((R, HID), bf16),
            pltpu.VMEM((R, HID), bf16),
            pltpu.VMEM((HID, C), bf16),
            pltpu.VMEM((2, NCH, R, CH), bf16),
            pltpu.VMEM((NCH, R, CH), bf16),
            pltpu.VMEM((SEG, HID, C), bf16),
            pltpu.VMEM((2, SEG, HID, C), bf16),
            pltpu.VMEM((R, TOK), f32),
            pltpu.VMEM((N, CAP, TOK), f32),
            pltpu.VMEM((N, TOK), f32),
            pltpu.VMEM((N, N, TOK), f32),
            dma((5 + NCH,)),
            dma((2, SEG, NCH)), dma((2, SEG, NCH)),
            dma((N,)), dma((N,)),
            dma((N,)), dma((N,)),
            dma((1,)), dma((3,)),
            dma((4,)), dma((4,)),
            dma((3, 2, 4)), dma((3, 2, 4)),
            dma((4,)), dma((4,)),
            dma((3,)), dma((3,)),
            dma((N,)), dma((N,)),
            dma((2, NCH)), dma((NCH,)),
            dma((NCH,)), dma((3, NCH)),
            dma((SEG, NCH)), dma((2, SEG, NCH)),
            dma((N,)), dma((N,)),
            dma((N,)), dma((N,)),
        ],
        compiler_params=pltpu.CompilerParams(
            collective_id=0, has_side_effects=True, vmem_limit_bytes=56 * 1024 * 1024
        ),
        cost_estimate=pl.CostEstimate(
            flops=4 * R * HID * C * N, bytes_accessed=6 * HID * C * 2, transcendentals=R * HID
        ),
    )(
        grad_out,
        routing.T,
        mix_weights.T,
        gate_pre.reshape(R, HID),
        up_pre.reshape(R, HID),
        down_weight.reshape(HID, C),
    )
    gg, gu, down, gm = pl.pallas_call(
        hand_out,
        out_shape=(
            jax.ShapeDtypeStruct((R, HID), bf16),
            jax.ShapeDtypeStruct((R, HID), bf16),
            jax.ShapeDtypeStruct((HID, C), bf16),
            jax.ShapeDtypeStruct((2, TOK), f32),
        ),
        in_specs=[hbm, hbm, hbm, vmem],
        out_specs=(hbm, hbm, hbm, vmem),
        scratch_shapes=[
            pltpu.VMEM((R, HID), bf16),
            pltpu.VMEM((R, HID), bf16),
            pltpu.VMEM((HID, C), bf16),
            dma((2, 3, 2)),
        ],
        compiler_params=pltpu.CompilerParams(vmem_limit_bytes=56 * 1024 * 1024),
    )(gg, gu, down, gm)
    return (
        gg.reshape(gate_pre.shape),
        gu.reshape(gate_pre.shape),
        gm.T,
        down[None],
    )


def solution(mesh):
    in_specs = (
        P(("dp", "expert"), "etp"),
        P(("dp", "expert"), None),
        P(("dp", "expert"), None),
        P("dp", "expert", None, None, "etp"),
        P("dp", "expert", None, None, "etp"),
        P("expert", "etp", "dp"),
    )
    out_specs = (
        P("dp", "expert", None, None, "etp"),
        P("dp", "expert", None, None, "etp"),
        P(("dp", "expert"), None),
        P("expert", "etp", "dp"),
    )
    return jax.shard_map(
        per_device, mesh=mesh, in_specs=in_specs, out_specs=out_specs, check_vma=False
    )
```
